32 devices in a mesh: outer: 8 (over z, x), inner: 4 (over y, core).
Axes of the slice: x: 2, y: 2, z: 4, core: 2. Of those that a mesh axis runs over, the one named last changes fastest.
Arguments:
- query_in: bfloat16 [4096, 1024], P(('outer', 'inner')), may hold values from -6 to 6
- key_in: bfloat16 [4096, 1024], P(('outer', 'inner')), may hold values from -6 to 6
- value_in: bfloat16 [4096, 1024], P(('outer', 'inner')), may hold values from -6 to 6
- conv_taps: float32 [3, 3, 1024], replicated, may hold values from -3.5 to 3.5
- long_filter: float32 [4096, 1024], P(('outer', 'inner')), may hold values from -1.1 to 1.1
- skip_gain: float32 [1024], replicated, may hold values from 0.5 to 1.5
- grad_out: bfloat16 [4096, 1024], P(('outer', 'inner')), may hold values from -6 to 6
Outputs:
- output: bfloat16 [4096, 1024], P(('outer', 'inner'))
- grad_query: bfloat16 [4096, 1024], P(('outer', 'inner'))
- grad_key: bfloat16 [4096, 1024], P(('outer', 'inner'))
- grad_value: bfloat16 [4096, 1024], P(('outer', 'inner'))
The draws below stay inside these ranges and needn't reach their ends.
All inputs are finite; a program needn't handle non-finite values.
Results may differ from the reference program's by a relative error of at most 0.001.
Values may be sent and summed in bfloat16 or wider, within the bound.
No kernel may reach another device: no remote copies, remote signals or barrier semaphores. Data moves between devices by JAX's collectives and lax.ppermute only.
A program may use at most 64 MiB of HBM per device.

```python
import math
import jax
import jax.numpy as jnp

CH = 1024
SEQ = 4096


def draw_long_filter(key, part):
    subkeys = jax.random.split(key, 4)
    position = jnp.arange(SEQ, dtype=jnp.int32)[:, None]
    distance = position.astype(jnp.float32)
    reaches = jnp.exp(jax.random.uniform(subkeys[0], (CH,), jnp.float32, math.log(30.0), math.log(4.0 * SEQ)))
    roughness = jnp.clip(jax.random.normal(subkeys[1], (SEQ, CH), jnp.float32), -4.0, 4.0)
    drop_places = jax.random.randint(subkeys[2], (3, CH), 0, SEQ)
    drop_sizes = jax.random.uniform(subkeys[3], (3, CH), jnp.float32, 0.5, 0.8)
    envelope = jnp.exp(-distance / reaches)
    for which_drop in range(3):
        envelope = envelope * jnp.where(position >= drop_places[which_drop], drop_sizes[which_drop], 1.0)
    normalizer = jnp.sqrt(2.0 / (reaches * (1.0 - jnp.exp(-2.0 * SEQ / reaches))))
    return roughness * envelope * normalizer


def level_of(stream_key, shape, cuts, smallest, top_value):
    level, own = 1.0, jax.random.fold_in(stream_key, 6)
    for axis_at, blocks in cuts:
        heights = jnp.exp(jax.random.uniform(jax.random.fold_in(own, axis_at), (blocks,), jnp.float32, smallest / len(cuts), top_value / len(cuts)))
        level = level * jnp.repeat(heights, shape[axis_at] // blocks).reshape([-1 if axis == axis_at else 1 for axis in range(len(shape))])
    return level


def bell_draw(rng, dims, spread, reach, cuts=(), held_as=jnp.bfloat16):
    values = spread * jax.random.normal(rng, dims, jnp.float32)
    if cuts:
        values = values * level_of(rng, dims, cuts, -0.22, 0.18)
    return jnp.clip(values, -reach, reach).astype(held_as)


def setup_inputs(seed: int = 0) -> dict:
    key_of = jax.random.split(jax.random.key(seed), 8)
    query_in = bell_draw(key_of[0], (SEQ, CH), 1.0, 6.0, ((0, 32),))
    key_in = bell_draw(key_of[1], (SEQ, CH), 1.0, 6.0, ((0, 32),))
    value_in = bell_draw(key_of[2], (SEQ, CH), 1.0, 6.0, ((0, 32),))
    conv_taps = bell_draw(key_of[3], (3, 3, CH), 3 ** -0.5, 3.5, (), jnp.float32)
    long_filter = draw_long_filter(jax.random.fold_in(key_of[7], 71), 0)
    skip_gain = jnp.clip(jax.random.uniform(key_of[5], (CH,), jnp.float32, 0.5, 1.5), 0.5, 1.5)
    grad_out = bell_draw(key_of[6], (SEQ, CH), 1.0, 6.0, ((0, 32),))
    return {"query_in": query_in, "key_in": key_in, "value_in": value_in, "conv_taps": conv_taps, "long_filter": long_filter, "skip_gain": skip_gain, "grad_out": grad_out}


def short_forward(stream, tap_set):
    padded = jnp.pad(stream, ((2, 0), (0, 0)))
    return tap_set[0] * stream + tap_set[1] * padded[1:-1] + tap_set[2] * padded[:-2]


def short_backward(grad_rows, tap_set):
    padded = jnp.pad(grad_rows, ((0, 2), (0, 0)))
    return tap_set[0] * grad_rows + tap_set[1] * padded[1:-1] + tap_set[2] * padded[2:]


def reference(query_in, key_in, value_in, conv_taps, long_filter, skip_gain, grad_out):
    length = query_in.shape[0]
    points = 2 * length
    short_q = short_forward(query_in.astype(jnp.float32), conv_taps[0])
    short_k = short_forward(key_in.astype(jnp.float32), conv_taps[1])
    short_v = short_forward(value_in.astype(jnp.float32), conv_taps[2])
    gated = short_k * short_v
    spec_filter = jnp.fft.rfft(long_filter, n=points, axis=0)
    spec_gated = jnp.fft.rfft(gated, n=points, axis=0)
    convolved = jnp.fft.irfft(spec_gated * spec_filter, n=points, axis=0)[:length]
    mixed = convolved + skip_gain * gated
    output = (short_q * mixed).astype(jnp.bfloat16)
    upstream = grad_out.astype(jnp.float32)
    grad_short_q = upstream * mixed
    grad_mixed = upstream * short_q
    spec_grad = jnp.fft.rfft(grad_mixed, n=points, axis=0)
    grad_gated = jnp.fft.irfft(jnp.conj(spec_filter) * spec_grad, n=points, axis=0)[:length] + skip_gain * grad_mixed
    grad_short_k = grad_gated * short_v
    grad_short_v = grad_gated * short_k
    grad_query = short_backward(grad_short_q, conv_taps[0]).astype(jnp.bfloat16)
    grad_key = short_backward(grad_short_k, conv_taps[1]).astype(jnp.bfloat16)
    grad_value = short_backward(grad_short_v, conv_taps[2]).astype(jnp.bfloat16)
    return (output, grad_query, grad_key, grad_value)
```

```python
import functools
import math

import jax
import jax.numpy as jnp
import ml_dtypes
import numpy as np
from jax import lax
from jax.experimental import pallas as pl
from jax.experimental.pallas import tpu as pltpu
from jax.sharding import PartitionSpec as P

AXES = ("outer", "inner")
f32 = jnp.float32
bf16 = jnp.bfloat16
VMEM_LIMIT = 56 * 1024 * 1024

OUTER_SLOPE = 4.0


class Code:
    def __init__(self, low, high, slope, top):
        self.low, self.high, self.slope = low, high, slope
        self.at_high = 126.0 - OUTER_SLOPE * (top - high)
        self.at_low = self.at_high - slope * (high - low)

    def encode(self, value):
        place = jnp.log2(jnp.abs(value))
        inside = jnp.clip(place, self.low, self.high)
        code = OUTER_SLOPE * place + ((self.slope - OUTER_SLOPE) * inside + self.shift())
        size = jnp.exp2(code)
        return jnp.where(value < 0, -size, size)

    def decode(self, word):
        code = jnp.log2(jnp.abs(word))
        inside = jnp.clip(code, self.at_low, self.at_high)
        place = (1.0 / OUTER_SLOPE) * code + (
            (1.0 / self.slope - 1.0 / OUTER_SLOPE) * inside + self.back_shift()
        )
        size = jnp.exp2(place)
        return jnp.where(word < 0, -size, size)

    def shift(self):
        return self.at_high - self.slope * self.high

    def back_shift(self):
        return self.high - self.at_high / self.slope


def split_pair(value):
    high = value.astype(bf16)
    return high, (value - high.astype(f32)).astype(bf16)


def numpy_pair(value):
    high = value.astype(np.float32).astype(ml_dtypes.bfloat16)
    low = (value - high.astype(np.float64)).astype(np.float32).astype(ml_dtypes.bfloat16)
    return high, low


def dot(left, right):
    return jnp.dot(left, right, preferred_element_type=f32)


def dot_pair(left, right):
    return dot(left[0], right[0]) + (dot(left[0], right[1]) + dot(left[1], right[0]))


@functools.lru_cache(maxsize=None)
def tables(blocks, rows, unit):
    points = 2 * blocks * rows
    bins = np.arange(blocks) + 0.5
    angle = np.outer(bins, np.arange(blocks)) * (2 * math.pi / (2 * blocks))
    eye = np.eye(unit)
    coarse = np.concatenate([np.kron(np.cos(angle), eye), np.kron(-np.sin(angle), eye)], axis=0)
    coarse_back = np.concatenate(
        [np.kron(np.cos(angle).T, eye), np.kron(-np.sin(angle).T, eye)], axis=1
    ) * (2.0 / points)
    twist = np.repeat(np.outer(bins, np.arange(rows)) * (2 * math.pi / points), unit, axis=0)
    fine = np.outer(np.arange(rows), np.arange(rows)) * (2 * math.pi / rows)
    cos, sin = np.cos(fine), np.sin(fine)
    forward = np.block([[cos, -sin], [sin, cos]])
    backward = np.block([[cos, sin], [-sin, cos]])
    pairs = [numpy_pair(table) for table in (coarse, coarse_back, forward, backward)]
    flat = [half for pair in pairs for half in pair]
    return flat + [np.cos(twist).astype(np.float32), np.sin(twist).astype(np.float32)]


def shifted(stream, steps, rim):
    rolled = pltpu.roll(stream, steps, 0)
    row = lax.broadcasted_iota(jnp.int32, stream.shape, 0)
    if steps == 1:
        return jnp.where(row == 0, rim[1:2], rolled)
    return jnp.where(row == 0, rim[0:1], jnp.where(row == 1, rim[1:2], rolled))


def short_forward(stream, taps, which, rim):
    return (
        taps[3 * which : 3 * which + 1] * stream
        + taps[3 * which + 1 : 3 * which + 2] * shifted(stream, 1, rim)
        + taps[3 * which + 2 : 3 * which + 3] * shifted(stream, 2, rim)
    )


def ahead(rows, steps):
    count = rows.shape[0]
    rolled = pltpu.roll(rows, count - steps, 0)
    row = lax.broadcasted_iota(jnp.int32, rows.shape, 0)
    return jnp.where(row < count - steps, rolled, 0.0)


def gate_kernel(code, groups, q_ref, k_ref, v_ref, g_ref, h_ref, rim_ref, taps_ref, out_ref, held):
    rows, channels = q_ref.shape
    count = channels // groups
    chunk = min(128, count)
    for start in range(0, channels, chunk):
        lanes = pl.ds(start, chunk)
        taps = taps_ref[:, lanes]
        rim = rim_ref[:, lanes].astype(f32)
        short_q = short_forward(q_ref[:, lanes].astype(f32), taps, 0, rim[0:2])
        short_k = short_forward(k_ref[:, lanes].astype(f32), taps, 1, rim[2:4])
        short_v = short_forward(v_ref[:, lanes].astype(f32), taps, 2, rim[4:6])
        signals = (
            short_k * short_v,
            h_ref[:, lanes] * 32.0,
            g_ref[:, lanes].astype(f32) * short_q,
        )
        for which, signal in enumerate(signals):
            word = code.encode(signal).T
            if groups == 1:
                held[which, pl.ds(start, chunk), :] = word
            else:
                group, first = start // count, start % count // 8
                held[which, pl.ds(first, chunk // 8), pl.ds(8 * group, 8), :] = word.reshape(
                    chunk // 8, 8, rows
                )
    for which in range(3):
        out_ref[which] = held[which].reshape(channels, rows).astype(bf16)


def transform_kernel(code_in, code_out, groups, *refs):
    x_ref = refs[0]
    table_refs = refs[1:11]
    out_ref, held, back = refs[11:]
    channels, rows = x_ref.shape[1:]
    count = channels // groups
    for which in range(3):
        words = code_in.decode(x_ref[which].astype(f32))
        held[which] = words.reshape(held.shape[1:])

    def one_group(group):
        def take(which):
            if groups == 1:
                return held[which]
            return held[which, :, pl.ds(8 * group, 8), :].reshape(count, rows)

        coarse = (table_refs[0][...], table_refs[1][...])
        coarse_back = (table_refs[2][...], table_refs[3][...])
        forward = (table_refs[4][...], table_refs[5][...])
        backward = (table_refs[6][...], table_refs[7][...])
        cos, sin = table_refs[8][...], table_refs[9][...]
        stacked = jnp.concatenate([take(0), take(1), take(2)], axis=1)
        first = dot_pair(coarse, split_pair(stacked))
        spectra = []
        for which in range(3):
            real = first[:count, which * rows : (which + 1) * rows]
            imag = first[count:, which * rows : (which + 1) * rows]
            turned = jnp.concatenate([real * cos + imag * sin, imag * cos - real * sin], axis=1)
            spectrum = dot_pair(split_pair(turned), forward)
            spectra.append((spectrum[:, :rows], spectrum[:, rows:]))
        (gr, gi), (hr, hi), (mr, mi) = spectra
        products = (
            (gr * hr - gi * hi, gr * hi + gi * hr),
            (mr * hr + mi * hi, mi * hr - mr * hi),
        )
        lasts = []
        for real, imag in products:
            product = jnp.concatenate([real, imag], axis=1)
            plain = dot_pair(split_pair(product), backward)
            real, imag = plain[:, :rows], plain[:, rows:]
            lasts.append(
                jnp.concatenate([real * cos - imag * sin, imag * cos + real * sin], axis=0)
            )
        result = dot_pair(coarse_back, split_pair(jnp.concatenate(lasts, axis=1)))
        result = result * (1.0 / 32.0)
        for which in range(2):
            part = result[:, which * rows : (which + 1) * rows]
            if groups == 1:
                back[which] = part
            else:
                back[which, :, pl.ds(8 * group, 8), :] = part.reshape(count // 8, 8, rows)

    for group in range(groups):
        one_group(group)
    for which in range(2):
        out_ref[which] = code_out.encode(back[which].reshape(channels, rows)).astype(bf16)


def finish_kernel(
    code,
    groups,
    y_ref,
    q_ref,
    k_ref,
    v_ref,
    g_ref,
    rim_ref,
    taps_ref,
    skip_ref,
    out_ref,
    gq_ref,
    gk_ref,
    gv_ref,
    first_ref,
    last_ref,
    held,
):
    rows, channels = q_ref.shape
    count = channels // groups
    chunk = min(128, count)
    for which in range(2):
        held[which] = code.decode(y_ref[which].astype(f32)).reshape(held.shape[1:])
    for start in range(0, channels, chunk):
        lanes = pl.ds(start, chunk)
        taps = taps_ref[:, lanes]
        skip = skip_ref[:, lanes]
        rim = rim_ref[:, lanes].astype(f32)

        def arrived(which):
            if groups == 1:
                return held[which, pl.ds(start, chunk), :].T
            group, first = start // count, start % count // 8
            part = held[which, pl.ds(first, chunk // 8), pl.ds(8 * group, 8), :]
            return part.reshape(chunk, rows).T

        short_q = short_forward(q_ref[:, lanes].astype(f32), taps, 0, rim[0:2])
        short_k = short_forward(k_ref[:, lanes].astype(f32), taps, 1, rim[2:4])
        short_v = short_forward(v_ref[:, lanes].astype(f32), taps, 2, rim[4:6])
        upstream = g_ref[:, lanes].astype(f32)
        mixed = arrived(0) + skip * (short_k * short_v)
        out_ref[:, lanes] = (short_q * mixed).astype(bf16)
        grad_gated = arrived(1) + skip * (upstream * short_q)
        grads = (upstream * mixed, grad_gated * short_v, grad_gated * short_k)
        for which, (rows_of, ref) in enumerate(zip(grads, (gq_ref, gk_ref, gv_ref))):
            total = (
                taps[3 * which : 3 * which + 1] * rows_of
                + taps[3 * which + 1 : 3 * which + 2] * ahead(rows_of, 1)
                + taps[3 * which + 2 : 3 * which + 3] * ahead(rows_of, 2)
            )
            ref[:, lanes] = total.astype(bf16)
            first_ref[2 * which : 2 * which + 2, lanes] = rows_of[0:2]
            last_ref[2 * which : 2 * which + 2, lanes] = total[rows - 2 :]


def rim_kernel(gq_ref, gk_ref, gv_ref, last_ref, later_ref, taps_ref, oq_ref, ok_ref, ov_ref):
    block = gq_ref.shape[0]
    row = lax.broadcasted_iota(jnp.int32, gq_ref.shape, 0)
    pairs = ((gq_ref, oq_ref), (gk_ref, ok_ref), (gv_ref, ov_ref))
    for which, (ref, out) in enumerate(pairs):
        one, two = taps_ref[3 * which + 1 : 3 * which + 2], taps_ref[3 * which + 2 : 3 * which + 3]
        at = 2 * which
        upper = last_ref[at : at + 1] + two * later_ref[at : at + 1]
        lower = (
            last_ref[at + 1 : at + 2]
            + one * later_ref[at : at + 1]
            + two * later_ref[at + 1 : at + 2]
        )
        value = ref[...].astype(f32)
        value = jnp.where(row == block - 2, upper, jnp.where(row == block - 1, lower, value))
        out[...] = value.astype(bf16)


def from_behind(value, steps):
    count = lax.axis_size(AXES)
    initial, last = max(0, -steps), min(count, count - steps)
    return lax.ppermute(value, AXES, [(at, at + steps) for at in range(initial, last)])


def local(query_in, key_in, value_in, conv_taps, long_filter, skip_gain, grad_out):
    rows, channels = query_in.shape
    blocks = lax.axis_size("inner") * lax.axis_size("outer")
    width = channels // blocks
    unit = 8 if width % 8 == 0 else width
    groups = width // unit
    code_in = Code(-7.0, 4.0, 16.0, 12.0)
    reach = math.ceil(math.log2(blocks * rows * 1.1 * 63.0 * 63.0))
    code_out = Code(-7.0, 4.0, 12.0, float(reach))
    params = pltpu.CompilerParams(vmem_limit_bytes=VMEM_LIMIT)
    taps = conv_taps.reshape(9, channels)
    skip = skip_gain.reshape(1, channels)
    held_shape = (channels, rows) if groups == 1 else (blocks, width, rows)

    rim = jnp.concatenate([query_in[rows - 2 :], key_in[rows - 2 :], value_in[rows - 2 :]], axis=0)
    earlier = from_behind(rim, 1)
    packed = pl.pallas_call(
        functools.partial(gate_kernel, code_in, groups),
        out_shape=jax.ShapeDtypeStruct((3, channels, rows), bf16),
        scratch_shapes=[pltpu.VMEM((3,) + held_shape, f32)],
        compiler_params=params,
        name="gate",
    )(query_in, key_in, value_in, grad_out, long_filter, earlier, taps)
    spread = lax.all_to_all(packed.reshape(3, blocks, width, rows), AXES, 1, 1, tiled=True)
    result = pl.pallas_call(
        functools.partial(transform_kernel, code_in, code_out, groups),
        out_shape=jax.ShapeDtypeStruct((2, channels, rows), bf16),
        scratch_shapes=[pltpu.VMEM((3,) + held_shape, f32), pltpu.VMEM((2,) + held_shape, f32)],
        compiler_params=params,
        name="transform",
    )(spread.reshape(3, channels, rows), *[jnp.asarray(t) for t in tables(blocks, rows, unit)])
    returned = lax.all_to_all(result.reshape(2, blocks, width, rows), AXES, 1, 1, tiled=True)
    wide = jax.ShapeDtypeStruct((rows, channels), bf16)
    narrow = jax.ShapeDtypeStruct((6, channels), f32)
    output, grad_q, grad_k, grad_v, first, last = pl.pallas_call(
        functools.partial(finish_kernel, code_out, groups),
        out_shape=(wide, wide, wide, wide, narrow, narrow),
        scratch_shapes=[pltpu.VMEM((2,) + held_shape, f32)],
        compiler_params=params,
        name="finish",
    )(
        returned.reshape(2, channels, rows),
        query_in,
        key_in,
        value_in,
        grad_out,
        earlier,
        taps,
        skip,
    )
    later = from_behind(first, -1)
    tail = pl.BlockSpec((16, channels), lambda step: (rows // 16 - 1, 0))
    whole = [pl.BlockSpec((size, channels), lambda step: (0, 0)) for size in (6, 6, 9)]
    grad_q, grad_k, grad_v = pl.pallas_call(
        rim_kernel,
        grid=(1,),
        out_shape=(wide, wide, wide),
        in_specs=[tail, tail, tail] + whole,
        out_specs=(tail, tail, tail),
        input_output_aliases={0: 0, 1: 1, 2: 2},
        compiler_params=params,
        name="rim",
    )(grad_q, grad_k, grad_v, last, later, taps)
    return output, grad_q, grad_k, grad_v


def solution(mesh):
    split = P(AXES, None)
    return jax.shard_map(
        local,
        mesh=mesh,
        in_specs=(split, split, split, P(), split, P(), split),
        out_specs=(split, split, split, split),
        check_vma=False,
    )
```

```python
import functools
import math

import jax
import jax.numpy as jnp
import ml_dtypes
import numpy as np
from jax import lax
from jax.experimental import pallas as pl
from jax.experimental.pallas import tpu as pltpu
from jax.sharding import PartitionSpec as P

AXES = ("outer", "inner")
f32 = jnp.float32
bf16 = jnp.bfloat16
ITEMS = 32

LOW, HIGH, STEEP, FLAT = -11.0, 0.25, 17.0, 4.0
AT_HIGH = 126.0
AT_LOW = AT_HIGH - STEEP * (HIGH - LOW)


def encode(value):
    place = jnp.log2(jnp.abs(value))
    inside = jnp.clip(place, LOW, HIGH)
    size = jnp.exp2(FLAT * place + ((STEEP - FLAT) * inside + (AT_HIGH - STEEP * HIGH)))
    return jnp.where(value < 0, -size, size)


def decode(word):
    code = jnp.log2(jnp.abs(word))
    inside = jnp.clip(code, AT_LOW, AT_HIGH)
    size = jnp.exp2(
        (1.0 / FLAT) * code + ((1.0 / STEEP - 1.0 / FLAT) * inside + (HIGH - AT_HIGH / STEEP))
    )
    return jnp.where(word < 0, -size, size)


def scale_of(peaks):
    top = jnp.max(jnp.max(peaks, axis=0, keepdims=True), axis=1, keepdims=True)
    return jnp.maximum(top, 2.0**-100).astype(bf16).astype(f32)


def peaks_of(value):
    rows, lanes = value.shape
    return jnp.max(jnp.abs(value).reshape(rows // 8, 8, lanes), axis=0)


def split_pair(value):
    high = value.astype(bf16)
    return high, (value - high.astype(f32)).astype(bf16)


def numpy_pair(value):
    high = value.astype(np.float32).astype(ml_dtypes.bfloat16)
    low = (value - high.astype(np.float64)).astype(np.float32).astype(ml_dtypes.bfloat16)
    return high, low


def table_on_left(table, value):
    high, low = split_pair(value)
    return jnp.dot(table, jnp.concatenate([high, low, high], axis=0), preferred_element_type=f32)


def table_on_right(value, table):
    high, low = split_pair(value)
    return jnp.dot(jnp.concatenate([high, high, low], axis=1), table, preferred_element_type=f32)


@functools.lru_cache(maxsize=None)
def tables(blocks, rows, unit):
    points = 2 * blocks * rows
    bins = np.arange(blocks) + 0.5
    angle = np.outer(bins, np.arange(blocks)) * (2 * math.pi / (2 * blocks))
    eye = np.eye(unit)
    coarse = np.concatenate([np.kron(np.cos(angle), eye), np.kron(-np.sin(angle), eye)], axis=0)
    coarse_back = np.concatenate(
        [np.kron(np.cos(angle).T, eye), np.kron(-np.sin(angle).T, eye)], axis=1
    ) * (2.0 / points)
    twist = np.repeat(np.outer(bins, np.arange(rows)) * (2 * math.pi / points), unit, axis=0)
    fine = np.outer(np.arange(rows), np.arange(rows)) * (2 * math.pi / rows)
    cos, sin = np.cos(fine), np.sin(fine)
    forward = np.block([[cos, -sin], [sin, cos]])
    backward = np.block([[cos, sin], [-sin, cos]])
    flat = []
    for table in (coarse, coarse_back):
        high, low = numpy_pair(table)
        flat.append(np.concatenate([high, high, low], axis=1))
    for table in (forward, backward):
        high, low = numpy_pair(table)
        flat.append(np.concatenate([high, low, high], axis=0))
    return flat + [np.cos(twist).astype(np.float32), np.sin(twist).astype(np.float32)]


def shifted(stream, steps, rim):
    rolled = pltpu.roll(stream, steps, 0)
    if rim is None:
        return rolled
    row = lax.broadcasted_iota(jnp.int32, stream.shape, 0)
    if steps == 1:
        return jnp.where(row == 0, rim[1:2], rolled)
    return jnp.where(row == 0, rim[0:1], jnp.where(row == 1, rim[1:2], rolled))


def short_forward(stream, taps, which, rim):
    at = 3 * which
    return (
        taps[at : at + 1] * stream
        + taps[at + 1 : at + 2] * shifted(stream, 1, rim)
        + taps[at + 2 : at + 3] * shifted(stream, 2, rim)
    )


def short_after(stream, following, taps, which):
    at, rows = 3 * which, stream.shape[0]
    window = jnp.concatenate([stream[rows - 2 :], following], axis=0)
    return (
        taps[at : at + 1] * window[2:4]
        + taps[at + 1 : at + 2] * window[1:3]
        + taps[at + 2 : at + 3] * window[0:2]
    )


def ahead(rows, steps, rim):
    count = rows.shape[0]
    rolled = pltpu.roll(rows, count - steps, 0)
    row = lax.broadcasted_iota(jnp.int32, rows.shape, 0)
    if steps == 1:
        return jnp.where(row == count - 1, rim[0:1], rolled)
    return jnp.where(row == count - 2, rim[0:1], jnp.where(row == count - 1, rim[1:2], rolled))


def gate_kernel(groups, q_ref, k_ref, v_ref, g_ref, h_ref, taps_ref, out_ref, held, extra):
    rows, channels = q_ref.shape
    blocks = out_ref.shape[0]
    count = channels // groups
    unit = count // blocks
    width = unit * groups
    chunk = min(128, count)
    peaks = [None, None, None]
    extra[...] = jnp.zeros(extra.shape, f32)
    for start in range(0, channels, chunk):
        lanes = pl.ds(start, chunk)
        group, first = start // count, start % count // unit
        taps = taps_ref[:, lanes]
        query, key = q_ref[:, lanes].astype(f32), k_ref[:, lanes].astype(f32)
        value, upstream = v_ref[:, lanes].astype(f32), g_ref[:, lanes].astype(f32)
        for at, stream in enumerate((key, value, query, upstream)):
            extra[2 * at : 2 * at + 2, lanes] = stream[0:2]
        for at, stream in enumerate((key, value, query)):
            extra[8 + 2 * at : 10 + 2 * at, lanes] = stream[rows - 2 :]
        short_q = short_forward(query, taps, 0, None)
        short_k = short_forward(key, taps, 1, None)
        short_v = short_forward(value, taps, 2, None)
        for which, signal in enumerate((short_k * short_v, h_ref[:, lanes], upstream * short_q)):
            peak = peaks_of(signal)
            peaks[which] = peak if peaks[which] is None else jnp.maximum(peaks[which], peak)
            held[
                pl.ds(first, chunk // unit), pl.ds(which * width + group * unit, unit), :
            ] = signal.T.reshape(chunk // unit, unit, rows)
    for which in range(3):
        scale = scale_of(peaks[which])
        extra[14 + which : 15 + which, :] = jnp.broadcast_to(scale, (1, channels))
        part = pl.ds(which * width, width)
        out_ref[:, part, :] = encode(held[:, part, :] * (1.0 / scale)).astype(bf16)
    items = [extra[:, group * count : (group + 1) * count] for group in range(groups)]
    if ITEMS * groups < rows:
        items.append(jnp.zeros((rows - ITEMS * groups, count), f32))
    lines = jnp.concatenate(items, axis=0).T.reshape(blocks, unit, rows)
    out_ref[:, 3 * width :, :] = lines.astype(bf16)


def transform_kernel(groups, x_ref, own_ref, *refs):
    coarse_ref, coarse_back_ref, forward_ref, backward_ref, cos_ref, sin_ref = refs[:6]
    out_ref, held, back = refs[6:]
    blocks, lines, rows = x_ref.shape
    width = back.shape[1] // 2
    unit = width // groups
    count = blocks * unit
    held[...] = x_ref[...].astype(f32)

    extra = held[:, 3 * width :, :].reshape(count, rows)
    none = jnp.zeros((unit, rows), f32)
    before = jnp.concatenate([none, extra[: count - unit]], axis=0)
    after = jnp.concatenate([extra[unit:], none], axis=0)
    lane = lax.broadcasted_iota(jnp.int32, (count, rows), 1)
    item = lane % ITEMS

    def turn(value, steps):
        return value if steps % rows == 0 else pltpu.roll(value, steps % rows, 1)

    def own(tap):
        return jnp.broadcast_to(own_ref[tap][None], (blocks, unit, rows)).reshape(count, rows)

    middle = jnp.where(item % 2 == 0, turn(before, -9), turn(extra, 1))
    shorts = own(0) * extra + own(1) * middle + own(2) * turn(before, -8)
    edge_gated = shorts * turn(shorts, -2)
    edge_mixed = shorts * turn(extra, -2)

    def take(which, group):
        part = held[:, pl.ds(which * width + group * unit, unit), :].reshape(count, rows)
        signal = decode(part) * extra[:, 14 + which : 15 + which]
        if which == 1:
            return signal
        edge = (
            turn(edge_gated, -ITEMS * group)
            if which == 0
            else turn(edge_mixed, -ITEMS * group - 4)
        )
        return jnp.where(lane < 2, edge, signal)

    peaks = [None, None]
    together = 2 if groups % 2 == 0 else 1
    for base in range(0, groups, together):
        cos, sin = cos_ref[...], sin_ref[...]
        members = range(base, base + together)
        stacked = jnp.concatenate([take(which, g) for g in members for which in range(3)], axis=1)
        first = table_on_left(coarse_ref[...], stacked)
        lasts = []
        for at in range(together):
            spectra = []
            for which in range(3):
                here = slice((3 * at + which) * rows, (3 * at + which + 1) * rows)
                real, imag = first[:count, here], first[count:, here]
                turned = jnp.concatenate(
                    [real * cos + imag * sin, imag * cos - real * sin], axis=1
                )
                spectrum = table_on_right(turned, forward_ref[...])
                spectra.append((spectrum[:, :rows], spectrum[:, rows:]))
            (gr, gi), (hr, hi), (mr, mi) = spectra
            for real, imag in (
                (gr * hr - gi * hi, gr * hi + gi * hr),
                (mr * hr + mi * hi, mi * hr - mr * hi),
            ):
                product = jnp.concatenate([real, imag], axis=1)
                plain = table_on_right(product, backward_ref[...])
                real, imag = plain[:, :rows], plain[:, rows:]
                lasts.append(
                    jnp.concatenate([real * cos - imag * sin, imag * cos + real * sin], axis=0)
                )
        result = table_on_left(coarse_back_ref[...], jnp.concatenate(lasts, axis=1))
        for at, group in enumerate(members):
            for which in range(2):
                here = slice((2 * at + which) * rows, (2 * at + which + 1) * rows)
                part = result[:, here]
                peak = peaks_of(part)
                peaks[which] = peak if peaks[which] is None else jnp.maximum(peaks[which], peak)
                back[:, pl.ds(which * width + group * unit, unit), :] = part.reshape(
                    blocks, unit, rows
                )
    placed = jnp.zeros((count, rows), f32)
    for which in range(2):
        scale = scale_of(peaks[which])
        part = pl.ds(which * width, width)
        words = encode(back[:, part, :] * (1.0 / scale))
        out_ref[:, part, :] = words.astype(bf16)
        for group in range(groups):
            mine = words[:, group * unit : (group + 1) * unit, :].reshape(count, rows)
            at = ITEMS * group + 16 + 2 * which
            placed = jnp.where((lane >= at) & (lane < at + 2), turn(mine, at), placed)
        placed = jnp.where(item == 20 + which, scale, placed)
    following = jnp.concatenate([placed[unit:], none], axis=0)
    placed = jnp.where(item < 20, following, placed)
    lines = jnp.where(item < 8, after, jnp.where(item < 14, before, placed))
    out_ref[:, 2 * width :, :] = lines.reshape(blocks, unit, rows).astype(bf16)


def finish_kernel(groups, y_ref, q_ref, k_ref, v_ref, g_ref, taps_ref, skip_ref, *refs):
    out_ref, gq_ref, gk_ref, gv_ref, held = refs
    rows, channels = q_ref.shape
    blocks = y_ref.shape[0]
    count = channels // groups
    unit = count // blocks
    width = unit * groups
    chunk = min(128, count)
    held[...] = y_ref[...].astype(f32)
    extra = held[:, 2 * width :, :].reshape(count, rows).T
    for start in range(0, channels, chunk):
        lanes = pl.ds(start, chunk)
        group, first = start // count, start % count // unit
        taps = taps_ref[:, lanes]
        skip = skip_ref[:, lanes]
        inner = start % count
        items = extra[ITEMS * group : ITEMS * (group + 1), inner : inner + chunk]
        after = [items[2 * at : 2 * at + 2] for at in range(4)]
        before = [items[8 + 2 * at : 10 + 2 * at] for at in range(3)]

        def arrived(which):
            part = held[
                pl.ds(first, chunk // unit), pl.ds(which * width + group * unit, unit), :
            ].reshape(chunk, rows)
            scale = items[20 + which : 21 + which]
            return decode(part).T * scale, decode(items[16 + 2 * which : 18 + 2 * which]) * scale

        query, key = q_ref[:, lanes].astype(f32), k_ref[:, lanes].astype(f32)
        value, upstream = v_ref[:, lanes].astype(f32), g_ref[:, lanes].astype(f32)
        shorts = [
            (
                short_forward(stream, taps, which, before[at]),
                short_after(stream, after[at], taps, which),
            )
            for which, at, stream in ((0, 2, query), (1, 0, key), (2, 1, value))
        ]
        results = (arrived(0), arrived(1))
        upstreams = (upstream, after[3])
        grads = [[], [], []]
        for here in range(2):
            short_q, short_k, short_v = (short[here] for short in shorts)
            mixed = results[0][here] + skip * (short_k * short_v)
            if here == 0:
                out_ref[:, lanes] = (short_q * mixed).astype(bf16)
            grad_gated = results[1][here] + skip * (upstreams[here] * short_q)
            grads[0].append(upstreams[here] * mixed)
            grads[1].append(grad_gated * short_v)
            grads[2].append(grad_gated * short_k)
        for which, ref in enumerate((gq_ref, gk_ref, gv_ref)):
            rows_of, rim = grads[which]
            at = 3 * which
            ref[:, lanes] = (
                taps[at : at + 1] * rows_of
                + taps[at + 1 : at + 2] * ahead(rows_of, 1, rim)
                + taps[at + 2 : at + 3] * ahead(rows_of, 2, rim)
            ).astype(bf16)


def local(query_in, key_in, value_in, conv_taps, long_filter, skip_gain, grad_out):
    rows, channels = query_in.shape
    blocks = lax.axis_size("inner") * lax.axis_size("outer")
    width = channels // blocks
    unit = 8 if width % 8 == 0 else width
    groups = width // unit
    params = pltpu.CompilerParams(vmem_limit_bytes=(24 if unit == 8 else 56) * 1024 * 1024)
    taps = conv_taps.reshape(9, channels)
    skip = skip_gain.reshape(1, channels)

    own = conv_taps.reshape(3, 3, groups, blocks, unit)
    own = lax.dynamic_index_in_dim(own, lax.axis_index(AXES), 3, keepdims=False)
    own = jnp.stack([own[1], own[2], own[0]])
    own = jnp.repeat(jnp.transpose(own, (1, 3, 2, 0)), 2, axis=3)
    own = jnp.pad(own, ((0, 0), (0, 0), (0, 0), (0, ITEMS - 6))).reshape(3, unit, ITEMS * groups)
    own = jnp.pad(own, ((0, 0), (0, 0), (0, rows - ITEMS * groups)))

    lines = 3 * width + unit
    packed = pl.pallas_call(
        functools.partial(gate_kernel, groups),
        out_shape=jax.ShapeDtypeStruct((blocks, lines, rows), bf16),
        scratch_shapes=[
            pltpu.VMEM((blocks, 3 * width, rows), f32),
            pltpu.VMEM((ITEMS, channels), f32),
        ],
        compiler_params=params,
        name="gate",
    )(query_in, key_in, value_in, grad_out, long_filter, taps)
    spread = lax.all_to_all(packed, AXES, 0, 0, tiled=True)
    lines_back = 2 * width + unit
    result = pl.pallas_call(
        functools.partial(transform_kernel, groups),
        out_shape=jax.ShapeDtypeStruct((blocks, lines_back, rows), bf16),
        scratch_shapes=[
            pltpu.VMEM((blocks, lines, rows), f32),
            pltpu.VMEM((blocks, 2 * width, rows), f32),
        ],
        compiler_params=params,
        name="transform",
    )(spread, own, *[jnp.asarray(table) for table in tables(blocks, rows, unit)])
    returned = lax.all_to_all(result, AXES, 0, 0, tiled=True)
    wide = jax.ShapeDtypeStruct((rows, channels), bf16)
    return pl.pallas_call(
        functools.partial(finish_kernel, groups),
        out_shape=(wide, wide, wide, wide),
        scratch_shapes=[pltpu.VMEM((blocks, lines_back, rows), f32)],
        compiler_params=params,
        name="finish",
    )(returned, query_in, key_in, value_in, grad_out, taps, skip)


def solution(mesh):
    split = P(AXES, None)
    return jax.shard_map(
        local,
        mesh=mesh,
        in_specs=(split, split, split, P(), split, P(), split),
        out_specs=(split, split, split, split),
        check_vma=False,
    )
```

```python
import functools
import math

import jax
import jax.numpy as jnp
import ml_dtypes
import numpy as np
from jax import lax
from jax.experimental import pallas as pl
from jax.experimental.pallas import tpu as pltpu
from jax.sharding import PartitionSpec as P

AXES = ("outer", "inner")
f32 = jnp.float32
bf16 = jnp.bfloat16
ITEMS = 32

REACH = 240.0


def scale_of(top):
    return jnp.maximum(top, 2.0**-100).astype(bf16).astype(f32)


def encode(value, scale):
    power = value * (REACH / scale)
    sign = power < 0
    for _ in range(4):
        power = power * power
    return jnp.where(sign, -power, power)


def decode(word):
    size = jnp.exp2(jnp.log2(jnp.abs(word)) * (1.0 / 16.0))
    return jnp.where(word < 0, -size, size)


def split_pair(value):
    high = value.astype(bf16)
    return high, (value - high.astype(f32)).astype(bf16)


def numpy_pair(value):
    high = value.astype(np.float32).astype(ml_dtypes.bfloat16)
    low = (value - high.astype(np.float64)).astype(np.float32).astype(ml_dtypes.bfloat16)
    return high, low


def table_on_left(high_ref, low_ref, value):
    high, low = split_pair(value)
    table = jnp.concatenate([high_ref[...], high_ref[...], low_ref[...]], axis=1)
    return jnp.dot(table, jnp.concatenate([high, low, high], axis=0), preferred_element_type=f32)


def table_on_right(value, high_ref, low_ref):
    high, low = split_pair(value)
    table = jnp.concatenate([high_ref[...], low_ref[...], high_ref[...]], axis=0)
    return jnp.dot(jnp.concatenate([high, high, low], axis=1), table, preferred_element_type=f32)


@functools.lru_cache(maxsize=None)
def tables(blocks, rows, unit):
    points = 2 * blocks * rows
    bins = np.arange(blocks) + 0.5
    angle = np.outer(bins, np.arange(blocks)) * (2 * math.pi / (2 * blocks))
    eye = np.eye(unit)
    coarse = np.concatenate([np.kron(np.cos(angle), eye), np.kron(-np.sin(angle), eye)], axis=0)
    coarse_back = np.concatenate(
        [np.kron(np.cos(angle).T, eye), np.kron(-np.sin(angle).T, eye)], axis=1
    ) * (2.0 / points)
    twist = np.repeat(np.outer(bins, np.arange(rows)) * (2 * math.pi / points), unit, axis=0)
    fine = np.outer(np.arange(rows), np.arange(rows)) * (2 * math.pi / rows)
    cos, sin = np.cos(fine), np.sin(fine)
    forward = np.block([[cos, -sin], [sin, cos]])
    backward = np.block([[cos, sin], [-sin, cos]])
    flat = [half for table in (coarse, coarse_back, forward, backward) for half in numpy_pair(table)]
    return flat + [np.cos(twist).astype(np.float32), np.sin(twist).astype(np.float32)]


def shifted(stream, steps, rim):
    rolled = pltpu.roll(stream, steps, 0)
    if rim is None:
        return rolled
    row = lax.broadcasted_iota(jnp.int32, stream.shape, 0)
    if steps == 1:
        return jnp.where(row == 0, rim[1:2], rolled)
    return jnp.where(row == 0, rim[0:1], jnp.where(row == 1, rim[1:2], rolled))


def short_forward(stream, taps, rim):
    return taps[0] * stream + taps[1] * shifted(stream, 1, rim) + taps[2] * shifted(stream, 2, rim)


def short_after(stream, following, taps):
    window = jnp.concatenate([stream[stream.shape[0] - 2 :], following], axis=0)
    return taps[0] * window[2:4] + taps[1] * window[1:3] + taps[2] * window[0:2]


def taps_at(taps_ref, which, lanes):
    return [taps_ref[which, tap : tap + 1, lanes] for tap in range(3)]


def ahead(rows, steps, rim):
    count = rows.shape[0]
    rolled = pltpu.roll(rows, count - steps, 0)
    row = lax.broadcasted_iota(jnp.int32, rows.shape, 0)
    if steps == 1:
        return jnp.where(row == count - 1, rim[0:1], rolled)
    return jnp.where(row == count - 2, rim[0:1], jnp.where(row == count - 1, rim[1:2], rolled))


def gate_kernel(groups, q_ref, k_ref, v_ref, g_ref, h_ref, taps_ref, out_ref, extra):
    rows, channels = q_ref.shape
    blocks = out_ref.shape[0]
    count = channels // groups
    unit = count // blocks
    width = unit * groups
    chunk = min(128, count)
    together = 2 if groups % 2 == 0 else 1
    extra[14:ITEMS, :] = jnp.zeros((ITEMS - 14, channels), f32)

    def words(start):
        lanes = pl.ds(start, chunk)
        query, key = q_ref[:, lanes].astype(f32), k_ref[:, lanes].astype(f32)
        value, upstream = v_ref[:, lanes].astype(f32), g_ref[:, lanes].astype(f32)
        for at, stream in enumerate((key, value, query, upstream)):
            extra[2 * at : 2 * at + 2, lanes] = stream[0:2]
        for at, stream in enumerate((key, value, query)):
            extra[8 + 2 * at : 10 + 2 * at, lanes] = stream[rows - 2 :]
        short_q = short_forward(query, taps_at(taps_ref, 0, lanes), None)
        short_k = short_forward(key, taps_at(taps_ref, 1, lanes), None)
        short_v = short_forward(value, taps_at(taps_ref, 2, lanes), None)
        result = []
        row = lax.broadcasted_iota(jnp.int32, (8, chunk), 0)
        for which, signal in enumerate((short_k * short_v, h_ref[:, lanes], upstream * short_q)):
            if which != 1:
                edge = jnp.where(row < 2, 0.0, signal[:8])
                signal = jnp.concatenate([edge, signal[8:]], axis=0)
            scale = scale_of(jnp.max(jnp.abs(signal), axis=0, keepdims=True))
            extra[14 + which : 15 + which, lanes] = scale
            result.append(encode(signal, scale).T.reshape(chunk // unit, unit, rows))
        return result

    for base in range(0, groups, together):
        for inner in range(0, count, chunk):
            pieces = [words((base + at) * count + inner) for at in range(together)]
            for which in range(3):
                piece = jnp.concatenate([part[which] for part in pieces], axis=1)
                out_ref[
                    pl.ds(inner // unit, chunk // unit),
                    pl.ds(which * width + base * unit, together * unit),
                    :,
                ] = piece.astype(bf16)
    items = [extra[:, group * count : (group + 1) * count] for group in range(groups)]
    if ITEMS * groups < rows:
        items.append(jnp.zeros((rows - ITEMS * groups, count), f32))
    lines = jnp.concatenate(items, axis=0).T.reshape(blocks, unit, rows)
    out_ref[:, 3 * width :, :] = lines.astype(bf16)


def transform_kernel(groups, width, x_ref, own_ref, *refs):
    coarse, coarse_back, forward, backward = refs[0:2], refs[2:4], refs[4:6], refs[6:8]
    cos_ref, sin_ref, out_ref = refs[8:]
    blocks, lines, rows = x_ref.shape
    unit = width // groups
    count = blocks * unit
    together = 2 if groups % 2 == 0 else 1

    extra = x_ref[:, 3 * width :, :].astype(f32).reshape(count, rows)
    none = jnp.zeros((unit, rows), f32)
    before = jnp.concatenate([none, extra[: count - unit]], axis=0)
    after = jnp.concatenate([extra[unit:], none], axis=0)
    lane = lax.broadcasted_iota(jnp.int32, (count, rows), 1)
    item = lane % ITEMS

    def turn(value, steps):
        return value if steps % rows == 0 else pltpu.roll(value, steps % rows, 1)

    def own(tap):
        return jnp.broadcast_to(own_ref[tap][None], (blocks, unit, rows)).reshape(count, rows)

    middle = jnp.where(item % 2 == 0, turn(before, -9), turn(extra, 1))
    shorts = own(0) * extra + own(1) * middle + own(2) * turn(before, -8)
    edge_gated = shorts * turn(shorts, -2)
    edge_mixed = shorts * turn(extra, -2)

    def take(which, base):
        both = x_ref[:, pl.ds(which * width + base * unit, together * unit), :].astype(f32)
        signals = []
        for at in range(together):
            part = both[:, at * unit : (at + 1) * unit, :].reshape(count, rows)
            left = ITEMS * (base + at)
            scale = extra[:, left + 14 + which : left + 15 + which] * (1.0 / REACH)
            signal = decode(part) * scale
            if which == 0:
                signal = jnp.where(lane < 2, turn(edge_gated, -left), signal)
            if which == 2:
                signal = jnp.where(lane < 2, turn(edge_mixed, -left - 4), signal)
            signals.append(signal)
        return signals

    placed = jnp.zeros((count, rows), f32)
    for base in range(0, groups, together):
        cos, sin = cos_ref[...], sin_ref[...]
        taken = [take(which, base) for which in range(3)]
        stacked = jnp.concatenate(
            [taken[which][at] for at in range(together) for which in range(3)], axis=1
        )
        first = table_on_left(*coarse, stacked)
        lasts = []
        for at in range(together):
            spectra = []
            for which in range(3):
                here = slice((3 * at + which) * rows, (3 * at + which + 1) * rows)
                real, imag = first[:count, here], first[count:, here]
                turned = jnp.concatenate(
                    [real * cos + imag * sin, imag * cos - real * sin], axis=1
                )
                spectrum = table_on_right(turned, *forward)
                spectra.append((spectrum[:, :rows], spectrum[:, rows:]))
            (gr, gi), (hr, hi), (mr, mi) = spectra
            for real, imag in (
                (gr * hr - gi * hi, gr * hi + gi * hr),
                (mr * hr + mi * hi, mi * hr - mr * hi),
            ):
                product = jnp.concatenate([real, imag], axis=1)
                plain = table_on_right(product, *backward)
                real, imag = plain[:, :rows], plain[:, rows:]
                lasts.append(
                    jnp.concatenate([real * cos - imag * sin, imag * cos + real * sin], axis=0)
                )
        result = table_on_left(*coarse_back, jnp.concatenate(lasts, axis=1))
        for which in range(2):
            pieces = []
            for at in range(together):
                here = slice((2 * at + which) * rows, (2 * at + which + 1) * rows)
                part = result[:, here].reshape(blocks, unit, rows)
                scale = scale_of(
                    jnp.max(jnp.max(jnp.abs(part), axis=0), axis=1, keepdims=True)
                )
                words = encode(part, scale[None])
                pieces.append(words)
                left = ITEMS * (base + at) + 16 + 2 * which
                mine = turn(words.reshape(count, rows), left)
                placed = jnp.where((lane >= left) & (lane < left + 2), mine, placed)
                spot = ITEMS * (base + at) + 20 + which
                all_scale = jnp.broadcast_to(scale[None], (blocks, unit, rows))
                placed = jnp.where(lane == spot, all_scale.reshape(count, rows), placed)
            out_ref[:, pl.ds(which * width + base * unit, together * unit), :] = jnp.concatenate(
                pieces, axis=1
            ).astype(bf16)
    following = jnp.concatenate([placed[unit:], none], axis=0)
    placed = jnp.where(item < 20, following, placed)
    lines = jnp.where(item < 8, after, jnp.where(item < 14, before, placed))
    out_ref[:, 2 * width :, :] = lines.reshape(blocks, unit, rows).astype(bf16)


def finish_kernel(groups, y_ref, q_ref, k_ref, v_ref, g_ref, taps_ref, skip_ref, *refs):
    out_ref, gq_ref, gk_ref, gv_ref = refs
    rows, channels = q_ref.shape
    blocks = y_ref.shape[0]
    count = channels // groups
    unit = count // blocks
    width = unit * groups
    chunk = min(128, count)
    together = 2 if groups % 2 == 0 else 1
    extra = y_ref[:, 2 * width :, :].astype(f32).reshape(count, rows).T

    def one_chunk(group, inner, parts):
        start = group * count + inner
        lanes = pl.ds(start, chunk)
        skip = skip_ref[:, lanes]
        items = extra[ITEMS * group : ITEMS * (group + 1), inner : inner + chunk]
        after = [items[2 * at : 2 * at + 2] for at in range(4)]
        before = [items[8 + 2 * at : 10 + 2 * at] for at in range(3)]

        def arrived(which):
            scale = items[20 + which : 21 + which] * (1.0 / REACH)
            return (
                decode(parts[which]).T * scale,
                decode(items[16 + 2 * which : 18 + 2 * which]) * scale,
            )

        query, key = q_ref[:, lanes].astype(f32), k_ref[:, lanes].astype(f32)
        value, upstream = v_ref[:, lanes].astype(f32), g_ref[:, lanes].astype(f32)
        taps = [taps_at(taps_ref, which, lanes) for which in range(3)]
        shorts = [
            (
                short_forward(stream, taps[which], before[at]),
                short_after(stream, after[at], taps[which]),
            )
            for which, at, stream in ((0, 2, query), (1, 0, key), (2, 1, value))
        ]
        results = (arrived(0), arrived(1))
        upstreams = (upstream, after[3])
        grads = [[], [], []]
        for here in range(2):
            short_q, short_k, short_v = (short[here] for short in shorts)
            mixed = results[0][here] + skip * (short_k * short_v)
            if here == 0:
                out_ref[:, lanes] = (short_q * mixed).astype(bf16)
            grad_gated = results[1][here] + skip * (upstreams[here] * short_q)
            grads[0].append(upstreams[here] * mixed)
            grads[1].append(grad_gated * short_v)
            grads[2].append(grad_gated * short_k)
        for which, ref in enumerate((gq_ref, gk_ref, gv_ref)):
            rows_of, rim = grads[which]
            one, two, three = taps[which]
            ref[:, lanes] = (
                one * rows_of + two * ahead(rows_of, 1, rim) + three * ahead(rows_of, 2, rim)
            ).astype(bf16)

    for base in range(0, groups, together):
        for inner in range(0, count, chunk):
            both = [
                y_ref[
                    pl.ds(inner // unit, chunk // unit),
                    pl.ds(which * width + base * unit, together * unit),
                    :,
                ].astype(f32)
                for which in range(2)
            ]
            for at in range(together):
                parts = [
                    arrived[:, at * unit : (at + 1) * unit, :].reshape(chunk, rows)
                    for arrived in both
                ]
                one_chunk(base + at, inner, parts)


def local(query_in, key_in, value_in, conv_taps, long_filter, skip_gain, grad_out):
    rows, channels = query_in.shape
    blocks = lax.axis_size("inner") * lax.axis_size("outer")
    width = channels // blocks
    unit = 8 if width % 8 == 0 else width
    groups = width // unit
    large = pltpu.CompilerParams(vmem_limit_bytes=60 * 1024 * 1024)
    small = pltpu.CompilerParams(vmem_limit_bytes=24 * 1024 * 1024) if unit == 8 else large
    skip = skip_gain.reshape(1, channels)

    own = conv_taps.reshape(3, 3, groups, blocks, unit)
    own = lax.dynamic_index_in_dim(own, lax.axis_index(AXES), 3, keepdims=False)
    own = jnp.stack([own[1], own[2], own[0]])
    own = jnp.repeat(jnp.transpose(own, (1, 3, 2, 0)), 2, axis=3)
    own = jnp.pad(own, ((0, 0), (0, 0), (0, 0), (0, ITEMS - 6))).reshape(3, unit, ITEMS * groups)
    own = jnp.pad(own, ((0, 0), (0, 0), (0, rows - ITEMS * groups)))

    packed = pl.pallas_call(
        functools.partial(gate_kernel, groups),
        out_shape=jax.ShapeDtypeStruct((blocks, 3 * width + unit, rows), bf16),
        scratch_shapes=[pltpu.VMEM((ITEMS, channels), f32)],
        compiler_params=large,
        name="gate",
    )(query_in, key_in, value_in, grad_out, long_filter, conv_taps)
    spread = lax.all_to_all(packed, AXES, 0, 0, tiled=True)
    result = pl.pallas_call(
        functools.partial(transform_kernel, groups, width),
        out_shape=jax.ShapeDtypeStruct((blocks, 2 * width + unit, rows), bf16),
        compiler_params=small,
        name="transform",
    )(spread, own, *[jnp.asarray(table) for table in tables(blocks, rows, unit)])
    returned = lax.all_to_all(result, AXES, 0, 0, tiled=True)
    wide = jax.ShapeDtypeStruct((rows, channels), bf16)
    return pl.pallas_call(
        functools.partial(finish_kernel, groups),
        out_shape=(wide, wide, wide, wide),
        compiler_params=small,
        name="finish",
    )(returned, query_in, key_in, value_in, grad_out, conv_taps, skip)


def solution(mesh):
    split = P(AXES, None)
    return jax.shard_map(
        local,
        mesh=mesh,
        in_specs=(split, split, split, P(), split, P(), split),
        out_specs=(split, split, split, split),
        check_vma=False,
    )
```

```python
import functools
import math

import jax
import jax.numpy as jnp
import ml_dtypes
import numpy as np
from jax import lax
from jax.experimental import pallas as pl
from jax.experimental.pallas import tpu as pltpu
from jax.sharding import PartitionSpec as P

AXES = ("outer", "inner")
f32 = jnp.float32
bf16 = jnp.bfloat16
ITEMS = 32

REACH = 240.0


def scale_of(top):
    return jnp.maximum(top, 2.0**-100).astype(bf16).astype(f32)


def encode(value, scale):
    power = value * (REACH / scale)
    sign = power < 0
    for _ in range(4):
        power = power * power
    return jnp.where(sign, -power, power)


def decode(word):
    size = jnp.exp2(jnp.log2(jnp.abs(word)) * (1.0 / 16.0))
    return jnp.where(word < 0, -size, size)


def split_pair(value):
    high = value.astype(bf16)
    return high, (value - high.astype(f32)).astype(bf16)


def numpy_pair(value):
    high = value.astype(np.float32).astype(ml_dtypes.bfloat16)
    low = (value - high.astype(np.float64)).astype(np.float32).astype(ml_dtypes.bfloat16)
    return high, low


def table_on_left(high_table, low_table, value):
    high, low = split_pair(value)
    table = jnp.concatenate([high_table, high_table, low_table], axis=1)
    return jnp.dot(table, jnp.concatenate([high, low, high], axis=0), preferred_element_type=f32)


def table_on_right(value, high_table, low_table):
    high, low = split_pair(value)
    table = jnp.concatenate([high_table, low_table, high_table], axis=0)
    return jnp.dot(jnp.concatenate([high, high, low], axis=1), table, preferred_element_type=f32)


@functools.lru_cache(maxsize=None)
def tables(blocks, rows, unit):
    points = 2 * blocks * rows
    bins = np.arange(blocks) + 0.5
    angle = np.outer(bins, np.arange(blocks)) * (2 * math.pi / (2 * blocks))
    eye = np.eye(unit)
    coarse = np.concatenate([np.kron(np.cos(angle), eye), np.kron(-np.sin(angle), eye)], axis=0)
    coarse_back = np.concatenate(
        [np.kron(np.cos(angle).T, eye), np.kron(-np.sin(angle).T, eye)], axis=1
    ) * (2.0 / points)
    twist = np.repeat(np.outer(bins, np.arange(rows)) * (2 * math.pi / points), unit, axis=0)
    fine = np.outer(np.arange(rows), np.arange(rows)) * (2 * math.pi / rows)
    cos, sin = np.cos(fine), np.sin(fine)
    forward = np.block([[cos, -sin], [sin, cos]])
    backward = np.block([[cos, sin], [-sin, cos]])
    columns = 2 * rows
    twists = np.concatenate([np.cos(twist), np.sin(twist)], axis=1)
    flat = []
    for table in (coarse, coarse_back, forward, backward, twists):
        for half in numpy_pair(table):
            flat += np.split(half, table.shape[1] // columns, axis=1)
    return np.concatenate(flat)


def unpack_tables(ref, count, rows):
    columns = 2 * rows
    shapes = [(2 * count, count)] * 2 + [(count, 2 * count)] * 2 + [(columns, columns)] * 4
    shapes += [(count, columns)] * 2
    found, at = [], 0
    for height, length in shapes:
        parts = []
        for _ in range(length // columns):
            parts.append(ref[at : at + height])
            at += height
        found.append(jnp.concatenate(parts, axis=1) if len(parts) > 1 else parts[0])
    twists = found[8].astype(f32) + found[9].astype(f32)
    return found[0:2], found[2:4], found[4:6], found[6:8], twists[:, :rows], twists[:, rows:]


def shifted(stream, steps, rim):
    rolled = pltpu.roll(stream, steps, 0)
    if rim is None:
        return rolled
    edge = rolled[:8]
    row = lax.broadcasted_iota(jnp.int32, edge.shape, 0)
    for at in range(steps):
        edge = jnp.where(row == at, rim[2 - steps + at : 3 - steps + at], edge)
    return jnp.concatenate([edge, rolled[8:]], axis=0)


def short_forward(stream, taps, rim):
    return taps[0] * stream + taps[1] * shifted(stream, 1, rim) + taps[2] * shifted(stream, 2, rim)


def short_after(stream, following, taps):
    window = jnp.concatenate([stream[stream.shape[0] - 2 :], following], axis=0)
    return taps[0] * window[2:4] + taps[1] * window[1:3] + taps[2] * window[0:2]


def taps_at(taps_ref, which, lanes):
    return [taps_ref[which, tap : tap + 1, lanes] for tap in range(3)]


def ahead(rows, steps, rim):
    count = rows.shape[0]
    rolled = pltpu.roll(rows, count - steps, 0)
    edge = rolled[count - 8 :]
    row = lax.broadcasted_iota(jnp.int32, edge.shape, 0)
    for at in range(steps):
        edge = jnp.where(row == 8 - steps + at, rim[at : at + 1], edge)
    return jnp.concatenate([rolled[: count - 8], edge], axis=0)


def slices_of(channels):
    size = min(256, channels)
    return [pl.ds(start, size) for start in range(0, channels, size)]


def gate_kernel(unit, q_hbm, k_hbm, v_hbm, g_hbm, h_hbm, taps_hbm, out_hbm, *scratch):
    q_ref, k_ref, v_ref, g_ref, h_ref, taps_ref, out_ref, extra, sems, out_sems = scratch
    rows, channels = q_ref.shape
    blocks = out_ref.shape[0]
    width = channels // blocks
    run = min(width, 2 * unit)
    span = run * blocks
    chunk = 128
    starts = range(0, channels, chunk)
    pairs = (
        (taps_hbm, taps_ref),
        (k_hbm, k_ref),
        (v_hbm, v_ref),
        (q_hbm, q_ref),
        (g_hbm, g_ref),
        (h_hbm, h_ref),
    )
    copies = [
        pltpu.make_async_copy(hbm, ref, sems.at[at]) for at, (hbm, ref) in enumerate(pairs)
    ]
    for copy in copies:
        copy.start()
    extra[14:ITEMS, :] = jnp.zeros((ITEMS - 14, channels), f32)
    row = lax.broadcasted_iota(jnp.int32, (8, chunk), 0)

    def short(ref, tap_row, item, lanes):
        stream = ref[:, lanes].astype(f32)
        extra[2 * item : 2 * item + 2, lanes] = stream[0:2]
        extra[8 + 2 * item : 10 + 2 * item, lanes] = stream[rows - 2 :]
        return short_forward(stream, taps_at(taps_ref, tap_row, lanes), None)

    def send(which, start, signal):
        lanes = pl.ds(start, chunk)
        first, line = start % span // run, start // span * run
        if which != 1:
            edge = jnp.where(row < 2, 0.0, signal[:8])
            signal = jnp.concatenate([edge, signal[8:]], axis=0)
        scale = scale_of(jnp.max(jnp.abs(signal), axis=0, keepdims=True))
        extra[14 + which : 15 + which, lanes] = scale
        words = encode(signal, scale)
        if run % 16 == 0:
            words = words.astype(bf16).T.reshape(chunk // run, run, rows)
        else:
            words = words.T.reshape(chunk // run, run, rows).astype(bf16)
        out_ref[pl.ds(first, chunk // run), pl.ds(which * width + line, run), :] = words

    outs = []

    def leave(at, first, count):
        if run % 16 == 0:
            part = (slice(None), pl.ds(first, count))
            copy = pltpu.make_async_copy(out_ref.at[part], out_hbm.at[part], out_sems.at[at])
            copy.start()
            outs.append(copy)

    for copy in copies[:3]:
        copy.wait()
    for start in starts:
        lanes = pl.ds(start, chunk)
        send(0, start, short(k_ref, 1, 0, lanes) * short(v_ref, 2, 1, lanes))
    leave(0, 0, width)
    copies[3].wait()
    copies[4].wait()
    for start in starts:
        lanes = pl.ds(start, chunk)
        upstream = g_ref[:, lanes].astype(f32)
        extra[6:8, lanes] = upstream[0:2]
        send(2, start, upstream * short(q_ref, 0, 2, lanes))
    leave(2, 2 * width, width)
    copies[5].wait()
    for start in starts:
        send(1, start, h_ref[:, pl.ds(start, chunk)])
    leave(1, width, width)
    halves = run // unit
    items = []
    for start in range(0, channels, span):
        items += [extra[:, start : start + span]] * halves
    if ITEMS * len(items) < rows:
        items.append(jnp.zeros((rows - ITEMS * len(items), span), f32))
    lines = jnp.concatenate(items, axis=0).T.reshape(blocks, run, rows)
    lane = lax.broadcasted_iota(jnp.int32, (blocks, unit, rows), 2)
    merged = lines[:, :unit, :]
    for half in range(1, halves):
        part = lines[:, half * unit : (half + 1) * unit, :]
        merged = jnp.where(lane // ITEMS % halves == half, part, merged)
    out_ref[:, 3 * width :, :] = merged.astype(bf16)
    if run % 16 == 0:
        leave(3, 3 * width, unit)
    else:
        copy = pltpu.make_async_copy(out_ref, out_hbm, out_sems.at[0])
        copy.start()
        outs.append(copy)
    for copy in outs:
        copy.wait()


def transform_kernel(groups, width, x_ref, own_ref, table_ref, out_ref):
    blocks, lines, rows = x_ref.shape
    unit = width // groups
    count = blocks * unit
    coarse, coarse_back, forward, backward, cos, sin = unpack_tables(table_ref, count, rows)
    together = 2 if groups % 2 == 0 else 1

    extra = x_ref[:, 3 * width :, :].astype(f32).reshape(count, rows)
    none = jnp.zeros((unit, rows), f32)
    before = jnp.concatenate([none, extra[: count - unit]], axis=0)
    after = jnp.concatenate([extra[unit:], none], axis=0)
    lane = lax.broadcasted_iota(jnp.int32, (count, rows), 1)
    item = lane % ITEMS

    def turn(value, steps):
        return value if steps % rows == 0 else pltpu.roll(value, steps % rows, 1)

    def own(tap):
        return jnp.broadcast_to(own_ref[tap][None], (blocks, unit, rows)).reshape(count, rows)

    middle = jnp.where(item % 2 == 0, turn(before, -9), turn(extra, 1))
    shorts = own(0) * extra + own(1) * middle + own(2) * turn(before, -8)
    edge_gated = shorts * turn(shorts, -2)
    edge_mixed = shorts * turn(extra, -2)

    def take(which, base):
        both = x_ref[:, pl.ds(which * width + base * unit, together * unit), :].astype(f32)
        signals = []
        for at in range(together):
            part = both[:, at * unit : (at + 1) * unit, :].reshape(count, rows)
            left = ITEMS * (base + at)
            scale = extra[:, left + 14 + which : left + 15 + which] * (1.0 / REACH)
            signal = decode(part) * scale
            if which == 0:
                signal = jnp.where(lane < 2, turn(edge_gated, -left), signal)
            if which == 2:
                signal = jnp.where(lane < 2, turn(edge_mixed, -left - 4), signal)
            signals.append(signal)
        return signals

    placed = jnp.zeros((count, rows), f32)
    for base in range(0, groups, together):
        taken = [take(which, base) for which in range(3)]
        stacked = jnp.concatenate(
            [taken[which][at] for at in range(together) for which in range(3)], axis=1
        )
        first = table_on_left(*coarse, stacked)
        lasts = []
        for at in range(together):
            spectra = []
            for which in range(3):
                here = slice((3 * at + which) * rows, (3 * at + which + 1) * rows)
                real, imag = first[:count, here], first[count:, here]
                turned = jnp.concatenate(
                    [real * cos + imag * sin, imag * cos - real * sin], axis=1
                )
                spectrum = table_on_right(turned, *forward)
                spectra.append((spectrum[:, :rows], spectrum[:, rows:]))
            (gr, gi), (hr, hi), (mr, mi) = spectra
            for real, imag in (
                (gr * hr - gi * hi, gr * hi + gi * hr),
                (mr * hr + mi * hi, mi * hr - mr * hi),
            ):
                product = jnp.concatenate([real, imag], axis=1)
                plain = table_on_right(product, *backward)
                real, imag = plain[:, :rows], plain[:, rows:]
                lasts.append(
                    jnp.concatenate([real * cos - imag * sin, imag * cos + real * sin], axis=0)
                )
        result = table_on_left(*coarse_back, jnp.concatenate(lasts, axis=1))
        for which in range(2):
            pieces = []
            for at in range(together):
                here = slice((2 * at + which) * rows, (2 * at + which + 1) * rows)
                part = result[:, here].reshape(blocks, unit, rows)
                scale = scale_of(
                    jnp.max(jnp.max(jnp.abs(part), axis=0), axis=1, keepdims=True)
                )
                words = encode(part, scale[None])
                pieces.append(words)
                left = ITEMS * (base + at) + 16 + 2 * which
                mine = turn(words.reshape(count, rows), left)
                placed = jnp.where((lane >= left) & (lane < left + 2), mine, placed)
                spot = ITEMS * (base + at) + 20 + which
                all_scale = jnp.broadcast_to(scale[None], (blocks, unit, rows))
                placed = jnp.where(lane == spot, all_scale.reshape(count, rows), placed)
            out_ref[:, pl.ds(which * width + base * unit, together * unit), :] = jnp.concatenate(
                pieces, axis=1
            ).astype(bf16)
    following = jnp.concatenate([placed[unit:], none], axis=0)
    placed = jnp.where(item < 20, following, placed)
    lines = jnp.where(item < 8, after, jnp.where(item < 14, before, placed))
    out_ref[:, 2 * width :, :] = lines.reshape(blocks, unit, rows).astype(bf16)


def prepare_kernel(q_ref, k_ref, v_ref, taps_ref, short_ref, tail_ref, ready_ref):
    rows, channels = q_ref.shape
    chunk = 128
    none = jnp.zeros((2, chunk), f32)
    ready_ref[...] = jnp.ones(ready_ref.shape, f32)
    for start in range(0, channels, chunk):
        lanes = pl.ds(start, chunk)
        for which, ref in enumerate((q_ref, k_ref, v_ref)):
            stream = ref[:, lanes].astype(f32)
            tail_ref[which, :, lanes] = stream[rows - 8 :]
            short_ref[which, :, lanes] = short_forward(
                stream, taps_at(taps_ref, which, lanes), none
            )


def finish_kernel(
    unit, y_ref, g_ref, short_ref, tail_ref, taps_ref, skip_ref, *refs
):
    targets, held, sems = refs[:4], refs[4:8], refs[8]
    rows, channels = g_ref.shape
    blocks = y_ref.shape[0]
    width = channels // blocks
    run = min(width, 2 * unit)
    span = run * blocks
    chunk = 128
    halves = run // unit
    slices = slices_of(channels)
    copies = []
    extra = y_ref[:, 2 * width :, :].astype(f32).reshape(blocks * unit, rows)
    parts = [extra] + [pltpu.roll(extra, rows - half * ITEMS, 1) for half in range(1, halves)]
    parts = [part.reshape(blocks, unit, rows) for part in parts]
    extra = jnp.concatenate(parts, axis=1).reshape(span, rows).T
    row = lax.broadcasted_iota(jnp.int32, (8, chunk), 0)
    for start in range(0, channels, chunk):
        lanes = pl.ds(start, chunk)
        first, line = start % span // run, start // span * run
        skip = skip_ref[:, lanes]
        top, inner = start // span * halves * ITEMS, start % span
        items = extra[top : top + ITEMS, inner : inner + chunk]
        after = [items[2 * at : 2 * at + 2] for at in range(4)]
        before = [items[8 + 2 * at : 10 + 2 * at] for at in range(3)]

        def arrived(which):
            part = y_ref[pl.ds(first, chunk // run), pl.ds(which * width + line, run), :]
            if run % 16 == 0:
                part = part.reshape(chunk, rows).T.astype(f32)
            else:
                part = part.astype(f32).reshape(chunk, rows).T
            scale = items[20 + which : 21 + which] * (1.0 / REACH)
            return decode(part) * scale, decode(items[16 + 2 * which : 18 + 2 * which]) * scale

        upstream = g_ref[:, lanes].astype(f32)
        taps = [taps_at(taps_ref, which, lanes) for which in range(3)]
        shorts = []
        for which, at in ((0, 2), (1, 0), (2, 1)):
            one, two, three = taps[which]
            past = before[at]
            short = short_ref[which, :, lanes]
            edge = short[:8] + jnp.where(
                row == 0,
                two * past[1:2] + three * past[0:1],
                jnp.where(row == 1, three * past[1:2], 0.0),
            )
            tail = tail_ref[which, :, lanes]
            shorts.append(
                (
                    jnp.concatenate([edge, short[8:]], axis=0),
                    short_after(tail, after[at], taps[which]),
                )
            )
        results = (arrived(0), arrived(1))
        upstreams = (upstream, after[3])
        grads = [[], [], []]
        for here in range(2):
            short_q, short_k, short_v = (short[here] for short in shorts)
            mixed = results[0][here] + skip * (short_k * short_v)
            if here == 0:
                held[0][:, lanes] = (short_q * mixed).astype(bf16)
            grad_gated = results[1][here] + skip * (upstreams[here] * short_q)
            grads[0].append(upstreams[here] * mixed)
            grads[1].append(grad_gated * short_v)
            grads[2].append(grad_gated * short_k)
        for which in range(3):
            rows_of, rim = grads[which]
            one, two, three = taps[which]
            held[1 + which][:, lanes] = (
                one * rows_of + two * ahead(rows_of, 1, rim) + three * ahead(rows_of, 2, rim)
            ).astype(bf16)
        if (start + chunk) % slices[0].size == 0:
            at = start // slices[0].size
            for which in range(4):
                part = (slice(None), slices[at])
                copy = pltpu.make_async_copy(
                    held[which].at[part], targets[which].at[part], sems.at[at, which]
                )
                copy.start()
                copies.append(copy)
    for copy in copies:
        copy.wait()


def local(query_in, key_in, value_in, conv_taps, long_filter, skip_gain, grad_out):
    rows, channels = query_in.shape
    blocks = lax.axis_size("inner") * lax.axis_size("outer")
    width = channels // blocks
    unit = 8 if width % 8 == 0 else width
    groups = width // unit
    large = pltpu.CompilerParams(vmem_limit_bytes=60 * 1024 * 1024)
    small = pltpu.CompilerParams(vmem_limit_bytes=24 * 1024 * 1024) if unit == 8 else large
    skip = skip_gain.reshape(1, channels)

    run = min(width, 2 * unit)
    own = conv_taps.reshape(3, 3, width // run, blocks, run)
    own = lax.dynamic_index_in_dim(own, lax.axis_index(AXES), 3, keepdims=False)
    own = own.reshape(3, 3, groups, unit)
    own = jnp.stack([own[1], own[2], own[0]])
    own = jnp.repeat(jnp.transpose(own, (1, 3, 2, 0)), 2, axis=3)
    own = jnp.pad(own, ((0, 0), (0, 0), (0, 0), (0, ITEMS - 6))).reshape(3, unit, ITEMS * groups)
    own = jnp.pad(own, ((0, 0), (0, 0), (0, rows - ITEMS * groups)))

    far = pl.BlockSpec(memory_space=pltpu.HBM)
    near = pl.BlockSpec(memory_space=pltpu.VMEM)
    stream = pltpu.VMEM((rows, channels), bf16)
    parts = len(slices_of(channels))
    packed = pl.pallas_call(
        functools.partial(gate_kernel, unit),
        out_shape=jax.ShapeDtypeStruct((blocks, 3 * width + unit, rows), bf16),
        in_specs=[far] * 6,
        out_specs=far,
        scratch_shapes=[
            *[stream] * 4,
            pltpu.VMEM((rows, channels), f32),
            pltpu.VMEM((3, 3, channels), f32),
            pltpu.VMEM((blocks, 3 * width + unit, rows), bf16),
            pltpu.VMEM((ITEMS, channels), f32),
            pltpu.SemaphoreType.DMA((6,)),
            pltpu.SemaphoreType.DMA((4,)),
        ],
        compiler_params=large,
        name="gate",
    )(query_in, key_in, value_in, grad_out, long_filter, conv_taps)
    spread = lax.all_to_all(packed, AXES, 0, 0, tiled=True)
    short, tail, ready = pl.pallas_call(
        prepare_kernel,
        out_shape=(
            jax.ShapeDtypeStruct((3, rows, channels), f32),
            jax.ShapeDtypeStruct((3, 8, channels), f32),
            jax.ShapeDtypeStruct((unit, rows), f32),
        ),
        compiler_params=large,
        cost_estimate=pl.CostEstimate(
            flops=30 * rows * channels, bytes_accessed=20 * rows * channels, transcendentals=0
        ),
        name="prepare",
    )(query_in, key_in, value_in, conv_taps)
    result = pl.pallas_call(
        functools.partial(transform_kernel, groups, width),
        out_shape=jax.ShapeDtypeStruct((blocks, 2 * width + unit, rows), bf16),
        in_specs=[near, near, near],
        compiler_params=small,
        name="transform",
    )(spread, own * ready, jnp.asarray(tables(blocks, rows, unit)))
    returned = lax.all_to_all(result, AXES, 0, 0, tiled=True)
    wide = jax.ShapeDtypeStruct((rows, channels), bf16)
    return pl.pallas_call(
        functools.partial(finish_kernel, unit),
        out_shape=(wide, wide, wide, wide),
        in_specs=[near] * 6,
        out_specs=(far, far, far, far),
        scratch_shapes=[*[stream] * 4, pltpu.SemaphoreType.DMA((parts, 4))],
        compiler_params=small,
        name="finish",
    )(returned, grad_out, short, tail, conv_taps, skip)


def solution(mesh):
    split = P(AXES, None)
    return jax.shard_map(
        local,
        mesh=mesh,
        in_specs=(split, split, split, P(), split, P(), split),
        out_specs=(split, split, split, split),
        check_vma=False,
    )
```

```python
import functools
import math

import jax
import jax.numpy as jnp
import ml_dtypes
import numpy as np
from jax import lax
from jax.experimental import pallas as pl
from jax.experimental.pallas import tpu as pltpu
from jax.sharding import PartitionSpec as P

AXES = ("outer", "inner")
f32 = jnp.float32
bf16 = jnp.bfloat16
ITEMS = 32

REACH = 240.0


def scale_of(top):
    return jnp.maximum(top, 2.0**-100).astype(bf16).astype(f32)


def encode(value, scale):
    power = value * (REACH / scale)
    sign = power < 0
    for _ in range(4):
        power = power * power
    return jnp.where(sign, -power, power)


def decode(word):
    size = jnp.exp2(jnp.log2(jnp.abs(word)) * (1.0 / 16.0))
    return jnp.where(word < 0, -size, size)


def split_pair(value):
    high = value.astype(bf16)
    return high, (value - high.astype(f32)).astype(bf16)


def numpy_pair(value):
    high = value.astype(np.float32).astype(ml_dtypes.bfloat16)
    low = (value - high.astype(np.float64)).astype(np.float32).astype(ml_dtypes.bfloat16)
    return high, low


def table_on_left(table, value):
    high, low = split_pair(value)
    return jnp.dot(table, jnp.concatenate([high, low, high], axis=0), preferred_element_type=f32)


def table_on_right(value, high_table, low_table):
    high, low = split_pair(value)
    table = jnp.concatenate([high_table, low_table, high_table], axis=0)
    return jnp.dot(jnp.concatenate([high, high, low], axis=1), table, preferred_element_type=f32)


@functools.lru_cache(maxsize=None)
def tables(blocks, rows, unit):
    points = 2 * blocks * rows
    bins = 2 * np.arange(blocks // 4) + 1
    eye = np.eye(unit)
    coarse, coarse_back = [], []
    for which in range(4):
        angle = np.outer(bins, np.arange(which, blocks, 4)) * (math.pi / (2 * blocks))
        parts = [np.kron(np.cos(angle), eye), np.kron(-np.sin(angle), eye)]
        coarse.append(np.concatenate(parts, axis=0))
        coarse_back.append(np.concatenate([part.T for part in parts], axis=1) * (2.0 / points))
    signed = np.concatenate([bins, blocks + bins, bins - blocks, bins - 2 * blocks])
    twist = np.repeat(np.outer(signed, np.arange(rows)) * (math.pi / points), unit, axis=0)
    fine = np.outer(np.arange(rows), np.arange(rows)) * (2 * math.pi / rows)
    cos, sin = np.cos(fine), np.sin(fine)
    forward = np.block([[cos, -sin], [sin, cos]])
    backward = np.block([[cos, sin], [-sin, cos]])
    twists = np.concatenate([np.cos(twist), np.sin(twist)], axis=1)
    whole = []
    for table in coarse + coarse_back:
        high, low = numpy_pair(table)
        whole.append(np.concatenate([high, high, low], axis=1))
    for table in (forward, backward, twists):
        whole += numpy_pair(table)
    columns, flat = 2 * rows, []
    for table in whole:
        wide = np.pad(table, ((0, 0), (0, -table.shape[1] % columns)))
        flat += np.split(wide, wide.shape[1] // columns, axis=1)
    return np.concatenate(flat)


def unpack_tables(ref, count, rows):
    columns, quarter = 2 * rows, count // 4
    shapes = [(2 * quarter, 3 * quarter)] * 4 + [(quarter, 6 * quarter)] * 4
    shapes += [(columns, columns)] * 4 + [(count, columns)] * 2
    found, at = [], 0
    for height, length in shapes:
        parts = []
        for start in range(0, length, columns):
            parts.append(ref[at : at + height, : min(columns, length - start)])
            at += height
        found.append(jnp.concatenate(parts, axis=1) if len(parts) > 1 else parts[0])
    twists = found[12].astype(f32) + found[13].astype(f32)
    return found[:4], found[4:8], found[8:10], found[10:12], twists[:, :rows], twists[:, rows:]


def coarse_forward(coarse, value, blocks, unit):
    sums = []
    for which in range(4):
        places = range(which * unit, blocks * unit, 4 * unit)
        part = jnp.concatenate([value[at : at + unit] for at in places], axis=0)
        total = table_on_left(coarse[which], part)
        half = total.shape[0] // 2
        sums.append((total[:half], total[half:]))
    even = [left + right for left, right in zip(sums[0], sums[2])]
    even_less = [left - right for left, right in zip(sums[0], sums[2])]
    odd = [left + right for left, right in zip(sums[1], sums[3])]
    odd_less = [left - right for left, right in zip(sums[1], sums[3])]
    real = [even[0] + odd[0], even_less[0] + odd_less[1], even_less[0] - odd_less[1], even[0] - odd[0]]
    imag = [even[1] + odd[1], even_less[1] - odd_less[0], even_less[1] + odd_less[0], even[1] - odd[1]]
    return jnp.concatenate(real, axis=0), jnp.concatenate(imag, axis=0)


def coarse_backward(coarse_back, real, imag, blocks, unit):
    quarter = blocks * unit // 4
    real = [real[at * quarter : (at + 1) * quarter] for at in range(4)]
    imag = [imag[at * quarter : (at + 1) * quarter] for at in range(4)]
    outer_real, outer_imag = real[0] + real[3], imag[0] + imag[3]
    inner_real, inner_imag = real[1] + real[2], imag[1] + imag[2]
    outer_real_less, outer_imag_less = real[0] - real[3], imag[0] - imag[3]
    inner_real_less, inner_imag_less = real[1] - real[2], imag[1] - imag[2]
    mixes = (
        (outer_real + inner_real, outer_imag + inner_imag),
        (outer_real_less - inner_imag_less, outer_imag_less + inner_real_less),
        (outer_real - inner_real, outer_imag - inner_imag),
        (outer_real_less + inner_imag_less, outer_imag_less - inner_real_less),
    )
    results = [
        table_on_left(coarse_back[which], jnp.concatenate(mix, axis=0))
        for which, mix in enumerate(mixes)
    ]
    pieces = []
    for block in range(blocks):
        at = block // 4 * unit
        pieces.append(results[block % 4][at : at + unit])
    return jnp.concatenate(pieces, axis=0)


def shifted(stream, steps, rim):
    rolled = pltpu.roll(stream, steps, 0)
    if rim is None:
        return rolled
    edge = rolled[:8]
    row = lax.broadcasted_iota(jnp.int32, edge.shape, 0)
    for at in range(steps):
        edge = jnp.where(row == at, rim[2 - steps + at : 3 - steps + at], edge)
    return jnp.concatenate([edge, rolled[8:]], axis=0)


def short_forward(stream, taps, rim):
    return taps[0] * stream + taps[1] * shifted(stream, 1, rim) + taps[2] * shifted(stream, 2, rim)


def short_after(stream, following, taps):
    window = jnp.concatenate([stream[stream.shape[0] - 2 :], following], axis=0)
    return taps[0] * window[2:4] + taps[1] * window[1:3] + taps[2] * window[0:2]


def taps_at(taps_ref, which, lanes):
    return [taps_ref[which, tap : tap + 1, lanes] for tap in range(3)]


def ahead(rows, steps, rim):
    count = rows.shape[0]
    rolled = pltpu.roll(rows, count - steps, 0)
    edge = rolled[count - 8 :]
    row = lax.broadcasted_iota(jnp.int32, edge.shape, 0)
    for at in range(steps):
        edge = jnp.where(row == 8 - steps + at, rim[at : at + 1], edge)
    return jnp.concatenate([rolled[: count - 8], edge], axis=0)


def slices_of(channels):
    size = min(256, channels)
    return [pl.ds(start, size) for start in range(0, channels, size)]


def gate_kernel(unit, q_hbm, k_hbm, v_hbm, g_hbm, h_hbm, taps_hbm, out_hbm, *scratch):
    q_ref, k_ref, v_ref, g_ref, h_ref, taps_ref, out_ref, extra, sems, out_sems = scratch
    rows, channels = q_ref.shape
    blocks = out_ref.shape[0]
    width = channels // blocks
    run = min(width, 2 * unit)
    span = run * blocks
    chunk = 128
    starts = range(0, channels, chunk)
    pairs = (
        (taps_hbm, taps_ref),
        (k_hbm, k_ref),
        (v_hbm, v_ref),
        (q_hbm, q_ref),
        (g_hbm, g_ref),
        (h_hbm, h_ref),
    )
    copies = [
        pltpu.make_async_copy(hbm, ref, sems.at[at]) for at, (hbm, ref) in enumerate(pairs)
    ]
    for copy in copies:
        copy.start()
    extra[14:ITEMS, :] = jnp.zeros((ITEMS - 14, channels), f32)
    row = lax.broadcasted_iota(jnp.int32, (8, chunk), 0)

    def short(ref, tap_row, item, lanes):
        stream = ref[:, lanes].astype(f32)
        extra[2 * item : 2 * item + 2, lanes] = stream[0:2]
        extra[8 + 2 * item : 10 + 2 * item, lanes] = stream[rows - 2 :]
        return short_forward(stream, taps_at(taps_ref, tap_row, lanes), None)

    def send(which, start, signal):
        lanes = pl.ds(start, chunk)
        first, line = start % span // run, start // span * run
        if which != 1:
            edge = jnp.where(row < 2, 0.0, signal[:8])
            signal = jnp.concatenate([edge, signal[8:]], axis=0)
        scale = scale_of(jnp.max(jnp.abs(signal), axis=0, keepdims=True))
        extra[14 + which : 15 + which, lanes] = scale
        words = encode(signal, scale)
        if run % 16 == 0:
            words = words.astype(bf16).T.reshape(chunk // run, run, rows)
        else:
            words = words.T.reshape(chunk // run, run, rows).astype(bf16)
        out_ref[pl.ds(first, chunk // run), pl.ds(which * width + line, run), :] = words

    outs = []

    def leave(at, first, count):
        if run % 16 == 0:
            part = (slice(None), pl.ds(first, count))
            copy = pltpu.make_async_copy(out_ref.at[part], out_hbm.at[part], out_sems.at[at])
            copy.start()
            outs.append(copy)

    for copy in copies[:3]:
        copy.wait()
    for start in starts:
        lanes = pl.ds(start, chunk)
        send(0, start, short(k_ref, 1, 0, lanes) * short(v_ref, 2, 1, lanes))
    leave(0, 0, width)
    copies[3].wait()
    copies[4].wait()
    for start in starts:
        lanes = pl.ds(start, chunk)
        upstream = g_ref[:, lanes].astype(f32)
        extra[6:8, lanes] = upstream[0:2]
        send(2, start, upstream * short(q_ref, 0, 2, lanes))
    leave(2, 2 * width, width)
    copies[5].wait()
    for start in starts:
        send(1, start, h_ref[:, pl.ds(start, chunk)])
    leave(1, width, width)
    halves = run // unit
    items = []
    for start in range(0, channels, span):
        items += [extra[:, start : start + span]] * halves
    if ITEMS * len(items) < rows:
        items.append(jnp.zeros((rows - ITEMS * len(items), span), f32))
    lines = jnp.concatenate(items, axis=0).T.reshape(blocks, run, rows)
    lane = lax.broadcasted_iota(jnp.int32, (blocks, unit, rows), 2)
    merged = lines[:, :unit, :]
    for half in range(1, halves):
        part = lines[:, half * unit : (half + 1) * unit, :]
        merged = jnp.where(lane // ITEMS % halves == half, part, merged)
    out_ref[:, 3 * width :, :] = merged.astype(bf16)
    if run % 16 == 0:
        leave(3, 3 * width, unit)
    else:
        copy = pltpu.make_async_copy(out_ref, out_hbm, out_sems.at[0])
        copy.start()
        outs.append(copy)
    for copy in outs:
        copy.wait()


def transform_kernel(groups, width, x_ref, own_ref, table_ref, out_ref):
    blocks, lines, rows = x_ref.shape
    unit = width // groups
    count = blocks * unit
    coarse, coarse_back, forward, backward, cos, sin = unpack_tables(table_ref, count, rows)
    together = 2 if groups % 2 == 0 else 1

    extra = x_ref[:, 3 * width :, :].astype(f32).reshape(count, rows)
    none = jnp.zeros((unit, rows), f32)
    before = jnp.concatenate([none, extra[: count - unit]], axis=0)
    after = jnp.concatenate([extra[unit:], none], axis=0)
    lane = lax.broadcasted_iota(jnp.int32, (count, rows), 1)
    item = lane % ITEMS

    def turn(value, steps):
        return value if steps % rows == 0 else pltpu.roll(value, steps % rows, 1)

    def own(tap):
        return jnp.broadcast_to(own_ref[tap][None], (blocks, unit, rows)).reshape(count, rows)

    middle = jnp.where(item % 2 == 0, turn(before, -9), turn(extra, 1))
    shorts = own(0) * extra + own(1) * middle + own(2) * turn(before, -8)
    edge_gated = shorts * turn(shorts, -2)
    edge_mixed = shorts * turn(extra, -2)

    def take(which, base):
        both = x_ref[:, pl.ds(which * width + base * unit, together * unit), :].astype(f32)
        signals = []
        for at in range(together):
            part = both[:, at * unit : (at + 1) * unit, :].reshape(count, rows)
            left = ITEMS * (base + at)
            scale = extra[:, left + 14 + which : left + 15 + which] * (1.0 / REACH)
            signal = decode(part) * scale
            if which == 0:
                signal = jnp.where(lane < 2, turn(edge_gated, -left), signal)
            if which == 2:
                signal = jnp.where(lane < 2, turn(edge_mixed, -left - 4), signal)
            signals.append(signal)
        return signals

    placed = jnp.zeros((count, rows), f32)
    for base in range(0, groups, together):
        taken = [take(which, base) for which in range(3)]
        stacked = jnp.concatenate(
            [taken[which][at] for at in range(together) for which in range(3)], axis=1
        )
        first_real, first_imag = coarse_forward(coarse, stacked, blocks, unit)
        lasts = []
        for at in range(together):
            spectra = []
            for which in range(3):
                here = slice((3 * at + which) * rows, (3 * at + which + 1) * rows)
                real, imag = first_real[:, here], first_imag[:, here]
                turned = jnp.concatenate(
                    [real * cos + imag * sin, imag * cos - real * sin], axis=1
                )
                spectrum = table_on_right(turned, *forward)
                spectra.append((spectrum[:, :rows], spectrum[:, rows:]))
            (gr, gi), (hr, hi), (mr, mi) = spectra
            for real, imag in (
                (gr * hr - gi * hi, gr * hi + gi * hr),
                (mr * hr + mi * hi, mi * hr - mr * hi),
            ):
                product = jnp.concatenate([real, imag], axis=1)
                plain = table_on_right(product, *backward)
                real, imag = plain[:, :rows], plain[:, rows:]
                lasts.append((real * cos - imag * sin, imag * cos + real * sin))
        real, imag = (jnp.concatenate(parts, axis=1) for parts in zip(*lasts))
        result = coarse_backward(coarse_back, real, imag, blocks, unit)
        for which in range(2):
            pieces = []
            for at in range(together):
                here = slice((2 * at + which) * rows, (2 * at + which + 1) * rows)
                part = result[:, here].reshape(blocks, unit, rows)
                scale = scale_of(
                    jnp.max(jnp.max(jnp.abs(part), axis=0), axis=1, keepdims=True)
                )
                words = encode(part, scale[None])
                pieces.append(words)
                left = ITEMS * (base + at) + 16 + 2 * which
                mine = turn(words.reshape(count, rows), left)
                placed = jnp.where((lane >= left) & (lane < left + 2), mine, placed)
                spot = ITEMS * (base + at) + 20 + which
                all_scale = jnp.broadcast_to(scale[None], (blocks, unit, rows))
                placed = jnp.where(lane == spot, all_scale.reshape(count, rows), placed)
            out_ref[:, pl.ds(which * width + base * unit, together * unit), :] = jnp.concatenate(
                pieces, axis=1
            ).astype(bf16)
    following = jnp.concatenate([placed[unit:], none], axis=0)
    placed = jnp.where(item < 20, following, placed)
    lines = jnp.where(item < 8, after, jnp.where(item < 14, before, placed))
    out_ref[:, 2 * width :, :] = lines.reshape(blocks, unit, rows).astype(bf16)


def prepare_kernel(q_ref, k_ref, v_ref, taps_ref, sq_ref, skv_ref, tail_ref, ready_ref):
    rows, channels = q_ref.shape
    chunk = 128
    none = jnp.zeros((2, chunk), f32)
    ready_ref[...] = jnp.ones(ready_ref.shape, f32)
    for start in range(0, channels, chunk):
        lanes = pl.ds(start, chunk)
        for which, ref in enumerate((q_ref, k_ref, v_ref)):
            stream = ref[:, lanes].astype(f32)
            tail_ref[which, :, lanes] = stream[rows - 8 :]
            target = sq_ref if which == 0 else skv_ref.at[which - 1]
            target[:, lanes] = short_forward(stream, taps_at(taps_ref, which, lanes), none)


def finish_kernel(
    unit, y_ref, g_ref, sq_ref, skv_ref, tail_ref, taps_ref, skip_ref, *refs
):
    targets, held, sems = refs[:4], refs[4:8], refs[8]
    rows, channels = g_ref.shape
    blocks = y_ref.shape[0]
    width = channels // blocks
    run = min(width, 2 * unit)
    span = run * blocks
    chunk = 128
    halves = run // unit
    slices = slices_of(channels)
    copies = []
    extra = y_ref[:, 2 * width :, :].astype(f32).reshape(blocks * unit, rows)
    parts = [extra] + [pltpu.roll(extra, rows - half * ITEMS, 1) for half in range(1, halves)]
    parts = [part.reshape(blocks, unit, rows) for part in parts]
    extra = jnp.concatenate(parts, axis=1).reshape(span, rows).T
    row = lax.broadcasted_iota(jnp.int32, (8, chunk), 0)
    for start in range(0, channels, chunk):
        lanes = pl.ds(start, chunk)
        first, line = start % span // run, start // span * run
        skip = skip_ref[:, lanes]
        top, inner = start // span * halves * ITEMS, start % span
        items = extra[top : top + ITEMS, inner : inner + chunk]
        after = [items[2 * at : 2 * at + 2] for at in range(4)]
        before = [items[8 + 2 * at : 10 + 2 * at] for at in range(3)]

        def arrived(which):
            part = y_ref[pl.ds(first, chunk // run), pl.ds(which * width + line, run), :]
            if run % 16 == 0:
                part = part.reshape(chunk, rows).T.astype(f32)
            else:
                part = part.astype(f32).reshape(chunk, rows).T
            scale = items[20 + which : 21 + which] * (1.0 / REACH)
            return decode(part) * scale, decode(items[16 + 2 * which : 18 + 2 * which]) * scale

        upstream = g_ref[:, lanes].astype(f32)
        taps = [taps_at(taps_ref, which, lanes) for which in range(3)]
        shorts = []
        for which, at in ((0, 2), (1, 0), (2, 1)):
            one, two, three = taps[which]
            past = before[at]
            short = sq_ref[:, lanes] if which == 0 else skv_ref[which - 1, :, lanes]
            edge = short[:8] + jnp.where(
                row == 0,
                two * past[1:2] + three * past[0:1],
                jnp.where(row == 1, three * past[1:2], 0.0),
            )
            tail = tail_ref[which, :, lanes]
            shorts.append(
                (
                    jnp.concatenate([edge, short[8:]], axis=0),
                    short_after(tail, after[at], taps[which]),
                )
            )
        results = (arrived(0), arrived(1))
        upstreams = (upstream, after[3])
        grads = [[], [], []]
        for here in range(2):
            short_q, short_k, short_v = (short[here] for short in shorts)
            mixed = results[0][here] + skip * (short_k * short_v)
            if here == 0:
                held[0][:, lanes] = (short_q * mixed).astype(bf16)
            grad_gated = results[1][here] + skip * (upstreams[here] * short_q)
            grads[0].append(upstreams[here] * mixed)
            grads[1].append(grad_gated * short_v)
            grads[2].append(grad_gated * short_k)
        for which in range(3):
            rows_of, rim = grads[which]
            one, two, three = taps[which]
            held[1 + which][:, lanes] = (
                one * rows_of + two * ahead(rows_of, 1, rim) + three * ahead(rows_of, 2, rim)
            ).astype(bf16)
        if (start + chunk) % slices[0].size == 0:
            at = start // slices[0].size
            for which in range(4):
                part = (slice(None), slices[at])
                copy = pltpu.make_async_copy(
                    held[which].at[part], targets[which].at[part], sems.at[at, which]
                )
                copy.start()
                copies.append(copy)
    for copy in copies:
        copy.wait()


def local(query_in, key_in, value_in, conv_taps, long_filter, skip_gain, grad_out):
    rows, channels = query_in.shape
    blocks = lax.axis_size("inner") * lax.axis_size("outer")
    width = channels // blocks
    unit = 8 if width % 8 == 0 else width
    groups = width // unit
    large = pltpu.CompilerParams(vmem_limit_bytes=60 * 1024 * 1024)
    small = pltpu.CompilerParams(vmem_limit_bytes=24 * 1024 * 1024) if unit == 8 else large
    skip = skip_gain.reshape(1, channels)

    run = min(width, 2 * unit)
    own = conv_taps.reshape(3, 3, width // run, blocks, run)
    own = lax.dynamic_index_in_dim(own, lax.axis_index(AXES), 3, keepdims=False)
    own = own.reshape(3, 3, groups, unit)
    own = jnp.stack([own[1], own[2], own[0]])
    own = jnp.repeat(jnp.transpose(own, (1, 3, 2, 0)), 2, axis=3)
    own = jnp.pad(own, ((0, 0), (0, 0), (0, 0), (0, ITEMS - 6))).reshape(3, unit, ITEMS * groups)
    own = jnp.pad(own, ((0, 0), (0, 0), (0, rows - ITEMS * groups)))

    far = pl.BlockSpec(memory_space=pltpu.HBM)
    near = pl.BlockSpec(memory_space=pltpu.VMEM)
    stream = pltpu.VMEM((rows, channels), bf16)
    parts = len(slices_of(channels))
    packed = pl.pallas_call(
        functools.partial(gate_kernel, unit),
        out_shape=jax.ShapeDtypeStruct((blocks, 3 * width + unit, rows), bf16),
        in_specs=[far] * 6,
        out_specs=far,
        scratch_shapes=[
            *[stream] * 4,
            pltpu.VMEM((rows, channels), f32),
            pltpu.VMEM((3, 3, channels), f32),
            pltpu.VMEM((blocks, 3 * width + unit, rows), bf16),
            pltpu.VMEM((ITEMS, channels), f32),
            pltpu.SemaphoreType.DMA((6,)),
            pltpu.SemaphoreType.DMA((4,)),
        ],
        compiler_params=large,
        name="gate",
    )(query_in, key_in, value_in, grad_out, long_filter, conv_taps)
    spread = lax.all_to_all(packed, AXES, 0, 0, tiled=True)
    *short, tail, ready = pl.pallas_call(
        prepare_kernel,
        out_shape=(
            jax.ShapeDtypeStruct((rows, channels), f32),
            jax.ShapeDtypeStruct((2, rows, channels), f32),
            jax.ShapeDtypeStruct((3, 8, channels), f32),
            jax.ShapeDtypeStruct((unit, rows), f32),
        ),
        compiler_params=large,
        cost_estimate=pl.CostEstimate(
            flops=30 * rows * channels, bytes_accessed=20 * rows * channels, transcendentals=0
        ),
        name="prepare",
    )(query_in, key_in, value_in, conv_taps)
    result = pl.pallas_call(
        functools.partial(transform_kernel, groups, width),
        out_shape=jax.ShapeDtypeStruct((blocks, 2 * width + unit, rows), bf16),
        in_specs=[near, near, near],
        compiler_params=small,
        name="transform",
    )(spread, own * ready, jnp.asarray(tables(blocks, rows, unit)))
    returned = lax.all_to_all(result, AXES, 0, 0, tiled=True)
    wide = jax.ShapeDtypeStruct((rows, channels), bf16)
    return pl.pallas_call(
        functools.partial(finish_kernel, unit),
        out_shape=(wide, wide, wide, wide),
        in_specs=[near] * 7,
        out_specs=(far, far, far, far),
        scratch_shapes=[*[stream] * 4, pltpu.SemaphoreType.DMA((parts, 4))],
        compiler_params=small,
        name="finish",
    )(returned, grad_out, *short, tail, conv_taps, skip)


def solution(mesh):
    split = P(AXES, None)
    return jax.shard_map(
        local,
        mesh=mesh,
        in_specs=(split, split, split, P(), split, P(), split),
        out_specs=(split, split, split, split),
        check_vma=False,
    )
```

```python
import functools
import math

import jax
import jax.numpy as jnp
import ml_dtypes
import numpy as np
from jax import lax
from jax.experimental import pallas as pl
from jax.experimental.pallas import tpu as pltpu
from jax.sharding import PartitionSpec as P

AXES = ("outer", "inner")
f32 = jnp.float32
bf16 = jnp.bfloat16
ITEMS = 32

REACH = 240.0


def scale_of(top):
    return jnp.maximum(top, 2.0**-100).astype(bf16).astype(f32)


def encode(value, scale):
    power = value * (REACH / scale)
    sign = power < 0
    for _ in range(4):
        power = power * power
    return jnp.where(sign, -power, power)


def decode(word):
    size = jnp.exp2(jnp.log2(jnp.abs(word)) * (1.0 / 16.0))
    return jnp.where(word < 0, -size, size)


def split_pair(value):
    high = value.astype(bf16)
    return high, (value - high.astype(f32)).astype(bf16)


def numpy_pair(value):
    high = value.astype(np.float32).astype(ml_dtypes.bfloat16)
    low = (value - high.astype(np.float64)).astype(np.float32).astype(ml_dtypes.bfloat16)
    return high, low


def table_on_left(table, value):
    high, low = split_pair(value)
    return jnp.dot(table, jnp.concatenate([high, low, high], axis=0), preferred_element_type=f32)


def table_on_right(value, high_table, low_table):
    high, low = split_pair(value)
    table = jnp.concatenate([high_table, low_table, high_table], axis=0)
    return jnp.dot(jnp.concatenate([high, high, low], axis=1), table, preferred_element_type=f32)


@functools.lru_cache(maxsize=None)
def tables(blocks, rows, unit):
    points = 2 * blocks * rows
    bins = 2 * np.arange(blocks // 4) + 1
    eye = np.eye(unit)
    coarse, coarse_back = [], []
    for which in range(4):
        angle = np.outer(bins, np.arange(which, blocks, 4)) * (math.pi / (2 * blocks))
        parts = [np.kron(np.cos(angle), eye), np.kron(-np.sin(angle), eye)]
        coarse.append(np.concatenate(parts, axis=0))
        coarse_back.append(np.concatenate([part.T for part in parts], axis=1) * (2.0 / points))
    signed = np.concatenate([bins, blocks + bins, bins - blocks, bins - 2 * blocks])
    twist = np.repeat(np.outer(signed, np.arange(rows)) * (math.pi / points), unit, axis=0)
    fine = np.outer(np.arange(rows), np.arange(rows)) * (2 * math.pi / rows)
    cos, sin = np.cos(fine), np.sin(fine)
    forward = np.block([[cos, -sin], [sin, cos]])
    backward = np.block([[cos, sin], [-sin, cos]])
    twists = np.concatenate([np.cos(twist), np.sin(twist)], axis=1)
    whole = []
    for table in coarse + coarse_back:
        high, low = numpy_pair(table)
        whole.append(np.concatenate([high, high, low], axis=1))
    for table in (forward, backward, twists):
        whole += numpy_pair(table)
    columns, flat = 2 * rows, []
    for table in whole:
        wide = np.pad(table, ((0, 0), (0, -table.shape[1] % columns)))
        flat += np.split(wide, wide.shape[1] // columns, axis=1)
    return np.concatenate(flat)


def unpack_tables(ref, count, rows):
    columns, quarter = 2 * rows, count // 4
    shapes = [(2 * quarter, 3 * quarter)] * 4 + [(quarter, 6 * quarter)] * 4
    shapes += [(columns, columns)] * 4 + [(count, columns)] * 2
    found, at = [], 0
    for height, length in shapes:
        parts = []
        for start in range(0, length, columns):
            parts.append(ref[at : at + height, : min(columns, length - start)])
            at += height
        found.append(jnp.concatenate(parts, axis=1) if len(parts) > 1 else parts[0])
    twists = found[12].astype(f32) + found[13].astype(f32)
    return found[:4], found[4:8], found[8:10], found[10:12], twists[:, :rows], twists[:, rows:]


def coarse_forward(coarse, value, blocks, unit):
    sums = []
    for which in range(4):
        places = range(which * unit, blocks * unit, 4 * unit)
        part = jnp.concatenate([value[at : at + unit] for at in places], axis=0)
        total = table_on_left(coarse[which], part)
        half = total.shape[0] // 2
        sums.append((total[:half], total[half:]))
    even = [left + right for left, right in zip(sums[0], sums[2])]
    even_less = [left - right for left, right in zip(sums[0], sums[2])]
    odd = [left + right for left, right in zip(sums[1], sums[3])]
    odd_less = [left - right for left, right in zip(sums[1], sums[3])]
    real = [even[0] + odd[0], even_less[0] + odd_less[1], even_less[0] - odd_less[1], even[0] - odd[0]]
    imag = [even[1] + odd[1], even_less[1] - odd_less[0], even_less[1] + odd_less[0], even[1] - odd[1]]
    return jnp.concatenate(real, axis=0), jnp.concatenate(imag, axis=0)


def coarse_backward(coarse_back, real, imag, blocks, unit):
    quarter = blocks * unit // 4
    real = [real[at * quarter : (at + 1) * quarter] for at in range(4)]
    imag = [imag[at * quarter : (at + 1) * quarter] for at in range(4)]
    outer_real, outer_imag = real[0] + real[3], imag[0] + imag[3]
    inner_real, inner_imag = real[1] + real[2], imag[1] + imag[2]
    outer_real_less, outer_imag_less = real[0] - real[3], imag[0] - imag[3]
    inner_real_less, inner_imag_less = real[1] - real[2], imag[1] - imag[2]
    mixes = (
        (outer_real + inner_real, outer_imag + inner_imag),
        (outer_real_less - inner_imag_less, outer_imag_less + inner_real_less),
        (outer_real - inner_real, outer_imag - inner_imag),
        (outer_real_less + inner_imag_less, outer_imag_less - inner_real_less),
    )
    results = [
        table_on_left(coarse_back[which], jnp.concatenate(mix, axis=0))
        for which, mix in enumerate(mixes)
    ]
    pieces = []
    for block in range(blocks):
        at = block // 4 * unit
        pieces.append(results[block % 4][at : at + unit])
    return jnp.concatenate(pieces, axis=0)


def shifted(stream, steps, rim):
    rolled = pltpu.roll(stream, steps, 0)
    if rim is None:
        return rolled
    edge = rolled[:8]
    row = lax.broadcasted_iota(jnp.int32, edge.shape, 0)
    for at in range(steps):
        edge = jnp.where(row == at, rim[2 - steps + at : 3 - steps + at], edge)
    return jnp.concatenate([edge, rolled[8:]], axis=0)


def short_forward(stream, taps, rim):
    return taps[0] * stream + taps[1] * shifted(stream, 1, rim) + taps[2] * shifted(stream, 2, rim)


def short_after(stream, following, taps):
    window = jnp.concatenate([stream[stream.shape[0] - 2 :], following], axis=0)
    return taps[0] * window[2:4] + taps[1] * window[1:3] + taps[2] * window[0:2]


def taps_at(taps_ref, which, lanes):
    return [taps_ref[which, tap : tap + 1, lanes] for tap in range(3)]


def ahead(rows, steps, rim):
    count = rows.shape[0]
    rolled = pltpu.roll(rows, count - steps, 0)
    edge = rolled[count - 8 :]
    row = lax.broadcasted_iota(jnp.int32, edge.shape, 0)
    for at in range(steps):
        edge = jnp.where(row == 8 - steps + at, rim[at : at + 1], edge)
    return jnp.concatenate([rolled[: count - 8], edge], axis=0)


def slices_of(channels):
    size = min(512, channels)
    return [pl.ds(start, size) for start in range(0, channels, size)]


def gate_kernel(unit, q_hbm, k_hbm, v_hbm, g_hbm, h_hbm, taps_hbm, out_hbm, *scratch):
    q_ref, k_ref, v_ref, g_ref, h_ref, taps_ref, out_ref, extra, sems, out_sems = scratch
    rows, channels = q_ref.shape
    blocks = out_ref.shape[0]
    width = channels // blocks
    run = min(width, 2 * unit)
    span = run * blocks
    chunk = 128
    pairs = (
        (taps_hbm, taps_ref),
        (k_hbm, k_ref),
        (v_hbm, v_ref),
        (q_hbm, q_ref),
        (g_hbm, g_ref),
        (h_hbm, h_ref),
    )
    copies = [
        pltpu.make_async_copy(hbm, ref, sems.at[at]) for at, (hbm, ref) in enumerate(pairs)
    ]
    for copy in copies:
        copy.start()
    extra[14:ITEMS, :] = jnp.zeros((ITEMS - 14, channels), f32)
    row = lax.broadcasted_iota(jnp.int32, (8, chunk), 0)

    def short(ref, tap_row, item, lanes):
        stream = ref[:, lanes].astype(f32)
        extra[2 * item : 2 * item + 2, lanes] = stream[0:2]
        extra[8 + 2 * item : 10 + 2 * item, lanes] = stream[rows - 2 :]
        return short_forward(stream, taps_at(taps_ref, tap_row, lanes), None)

    def send(which, start, signal):
        lanes = pl.ds(start, chunk)
        first, line = start % span // run, start // span * run
        if which != 1:
            edge = jnp.where(row < 2, 0.0, signal[:8])
            signal = jnp.concatenate([edge, signal[8:]], axis=0)
        scale = scale_of(jnp.max(jnp.abs(signal), axis=0, keepdims=True))
        extra[14 + which : 15 + which, lanes] = scale
        words = encode(signal, scale)
        if run % 16 == 0:
            words = words.astype(bf16).T.reshape(chunk // run, run, rows)
        else:
            words = words.T.reshape(chunk // run, run, rows).astype(bf16)
        out_ref[pl.ds(first, chunk // run), pl.ds(which * width + line, run), :] = words

    halves = run // unit
    waited = []

    def wait_for(*which):
        for at in which:
            if at not in waited:
                copies[at].wait()
                waited.append(at)

    outs = []
    for part in range(2):
        half_span = span // 2
        firsts = [at + part * half_span for at in range(0, channels, span)]
        starts = [first + at for first in firsts for at in range(0, half_span, chunk)]
        wait_for(0, 1, 2)
        for start in starts:
            lanes = pl.ds(start, chunk)
            send(0, start, short(k_ref, 1, 0, lanes) * short(v_ref, 2, 1, lanes))
        wait_for(3, 4)
        for start in starts:
            lanes = pl.ds(start, chunk)
            upstream = g_ref[:, lanes].astype(f32)
            extra[6:8, lanes] = upstream[0:2]
            send(2, start, upstream * short(q_ref, 0, 2, lanes))
        wait_for(5)
        for start in starts:
            send(1, start, h_ref[:, pl.ds(start, chunk)])
        items = []
        for first in firsts:
            items += [extra[:, first : first + half_span]] * halves
        if ITEMS * len(items) < rows:
            items.append(jnp.zeros((rows - ITEMS * len(items), half_span), f32))
        lines = jnp.concatenate(items, axis=0).T.reshape(blocks // 2, run, rows)
        lane = lax.broadcasted_iota(jnp.int32, (blocks // 2, unit, rows), 2)
        merged = lines[:, :unit, :]
        for half in range(1, halves):
            other = lines[:, half * unit : (half + 1) * unit, :]
            merged = jnp.where(lane // ITEMS % halves == half, other, merged)
        mine = pl.ds(part * (blocks // 2), blocks // 2)
        out_ref[mine, 3 * width :, :] = merged.astype(bf16)
        copy = pltpu.make_async_copy(out_ref.at[mine], out_hbm.at[mine], out_sems.at[part])
        copy.start()
        outs.append(copy)
    for copy in outs:
        copy.wait()


def transform_kernel(groups, width, x_ref, own_ref, table_ref, out_ref):
    blocks, lines, rows = x_ref.shape
    unit = width // groups
    count = blocks * unit
    coarse, coarse_back, forward, backward, cos, sin = unpack_tables(table_ref, count, rows)
    together = 2 if groups % 2 == 0 else 1

    extra = x_ref[:, 3 * width :, :].astype(f32).reshape(count, rows)
    none = jnp.zeros((unit, rows), f32)
    before = jnp.concatenate([none, extra[: count - unit]], axis=0)
    after = jnp.concatenate([extra[unit:], none], axis=0)
    lane = lax.broadcasted_iota(jnp.int32, (count, rows), 1)
    item = lane % ITEMS

    def turn(value, steps):
        return value if steps % rows == 0 else pltpu.roll(value, steps % rows, 1)

    def own(tap):
        return jnp.broadcast_to(own_ref[tap][None], (blocks, unit, rows)).reshape(count, rows)

    middle = jnp.where(item % 2 == 0, turn(before, -9), turn(extra, 1))
    shorts = own(0) * extra + own(1) * middle + own(2) * turn(before, -8)
    edge_gated = shorts * turn(shorts, -2)
    edge_mixed = shorts * turn(extra, -2)

    def take(which, base):
        both = x_ref[:, pl.ds(which * width + base * unit, together * unit), :].astype(f32)
        signals = []
        for at in range(together):
            part = both[:, at * unit : (at + 1) * unit, :].reshape(count, rows)
            left = ITEMS * (base + at)
            scale = extra[:, left + 14 + which : left + 15 + which] * (1.0 / REACH)
            signal = decode(part) * scale
            if which == 0:
                signal = jnp.where(lane < 2, turn(edge_gated, -left), signal)
            if which == 2:
                signal = jnp.where(lane < 2, turn(edge_mixed, -left - 4), signal)
            signals.append(signal)
        return signals

    placed = jnp.zeros((count, rows), f32)
    for base in range(0, groups, together):
        taken = [take(which, base) for which in range(3)]
        stacked = jnp.concatenate(
            [taken[which][at] for at in range(together) for which in range(3)], axis=1
        )
        first_real, first_imag = coarse_forward(coarse, stacked, blocks, unit)
        lasts = []
        for at in range(together):
            spectra = []
            for which in range(3):
                here = slice((3 * at + which) * rows, (3 * at + which + 1) * rows)
                real, imag = first_real[:, here], first_imag[:, here]
                turned = jnp.concatenate(
                    [real * cos + imag * sin, imag * cos - real * sin], axis=1
                )
                spectrum = table_on_right(turned, *forward)
                spectra.append((spectrum[:, :rows], spectrum[:, rows:]))
            (gr, gi), (hr, hi), (mr, mi) = spectra
            for real, imag in (
                (gr * hr - gi * hi, gr * hi + gi * hr),
                (mr * hr + mi * hi, mi * hr - mr * hi),
            ):
                product = jnp.concatenate([real, imag], axis=1)
                plain = table_on_right(product, *backward)
                real, imag = plain[:, :rows], plain[:, rows:]
                lasts.append((real * cos - imag * sin, imag * cos + real * sin))
        real, imag = (jnp.concatenate(parts, axis=1) for parts in zip(*lasts))
        result = coarse_backward(coarse_back, real, imag, blocks, unit)
        for which in range(2):
            pieces = []
            for at in range(together):
                here = slice((2 * at + which) * rows, (2 * at + which + 1) * rows)
                part = result[:, here].reshape(blocks, unit, rows)
                scale = scale_of(
                    jnp.max(jnp.max(jnp.abs(part), axis=0), axis=1, keepdims=True)
                )
                words = encode(part, scale[None])
                pieces.append(words)
                left = ITEMS * (base + at) + 16 + 2 * which
                mine = turn(words.reshape(count, rows), left)
                placed = jnp.where((lane >= left) & (lane < left + 2), mine, placed)
                spot = ITEMS * (base + at) + 20 + which
                all_scale = jnp.broadcast_to(scale[None], (blocks, unit, rows))
                placed = jnp.where(lane == spot, all_scale.reshape(count, rows), placed)
            out_ref[:, pl.ds(which * width + base * unit, together * unit), :] = jnp.concatenate(
                pieces, axis=1
            ).astype(bf16)
    following = jnp.concatenate([placed[unit:], none], axis=0)
    placed = jnp.where(item < 20, following, placed)
    lines = jnp.where(item < 8, after, jnp.where(item < 14, before, placed))
    out_ref[:, 2 * width :, :] = lines.reshape(blocks, unit, rows).astype(bf16)


def prepare_kernel(q_ref, k_ref, v_ref, taps_ref, sq_ref, skv_ref, tail_ref, ready_ref):
    rows, channels = q_ref.shape
    chunk = 128
    none = jnp.zeros((2, chunk), f32)
    ready_ref[...] = jnp.ones(ready_ref.shape, f32)
    for start in range(0, channels, chunk):
        lanes = pl.ds(start, chunk)
        for which, ref in enumerate((q_ref, k_ref, v_ref)):
            stream = ref[:, lanes].astype(f32)
            tail_ref[which, :, lanes] = stream[rows - 8 :]
            target = sq_ref if which == 0 else skv_ref.at[which - 1]
            target[:, lanes] = short_forward(stream, taps_at(taps_ref, which, lanes), none)


def finish_kernel(
    unit, y_ref, g_ref, sq_ref, skv_ref, tail_ref, taps_ref, skip_ref, *refs
):
    targets, held, sems = refs[:4], refs[4:8], refs[8]
    rows, channels = g_ref.shape
    blocks = y_ref.shape[0]
    width = channels // blocks
    run = min(width, 2 * unit)
    span = run * blocks
    chunk = 128
    halves = run // unit
    slices = slices_of(channels)
    copies = []
    extra = y_ref[:, 2 * width :, :].astype(f32).reshape(blocks * unit, rows)
    parts = [extra] + [pltpu.roll(extra, rows - half * ITEMS, 1) for half in range(1, halves)]
    parts = [part.reshape(blocks, unit, rows) for part in parts]
    extra = jnp.concatenate(parts, axis=1).reshape(span, rows).T
    row = lax.broadcasted_iota(jnp.int32, (8, chunk), 0)
    for start in range(0, channels, chunk):
        lanes = pl.ds(start, chunk)
        first, line = start % span // run, start // span * run
        skip = skip_ref[:, lanes]
        top, inner = start // span * halves * ITEMS, start % span
        items = extra[top : top + ITEMS, inner : inner + chunk]
        after = [items[2 * at : 2 * at + 2] for at in range(4)]
        before = [items[8 + 2 * at : 10 + 2 * at] for at in range(3)]

        def arrived(which):
            part = y_ref[pl.ds(first, chunk // run), pl.ds(which * width + line, run), :]
            if run % 16 == 0:
                part = part.reshape(chunk, rows).T.astype(f32)
            else:
                part = part.astype(f32).reshape(chunk, rows).T
            scale = items[20 + which : 21 + which] * (1.0 / REACH)
            return decode(part) * scale, decode(items[16 + 2 * which : 18 + 2 * which]) * scale

        upstream = g_ref[:, lanes].astype(f32)
        taps = [taps_at(taps_ref, which, lanes) for which in range(3)]
        shorts = []
        for which, at in ((0, 2), (1, 0), (2, 1)):
            one, two, three = taps[which]
            past = before[at]
            short = sq_ref[:, lanes] if which == 0 else skv_ref[which - 1, :, lanes]
            edge = short[:8] + jnp.where(
                row == 0,
                two * past[1:2] + three * past[0:1],
                jnp.where(row == 1, three * past[1:2], 0.0),
            )
            tail = tail_ref[which, :, lanes]
            shorts.append(
                (
                    jnp.concatenate([edge, short[8:]], axis=0),
                    short_after(tail, after[at], taps[which]),
                )
            )
        results = (arrived(0), arrived(1))
        upstreams = (upstream, after[3])
        grads = [[], [], []]
        for here in range(2):
            short_q, short_k, short_v = (short[here] for short in shorts)
            mixed = results[0][here] + skip * (short_k * short_v)
            if here == 0:
                held[0][:, lanes] = (short_q * mixed).astype(bf16)
            grad_gated = results[1][here] + skip * (upstreams[here] * short_q)
            grads[0].append(upstreams[here] * mixed)
            grads[1].append(grad_gated * short_v)
            grads[2].append(grad_gated * short_k)
        for which in range(3):
            rows_of, rim = grads[which]
            one, two, three = taps[which]
            held[1 + which][:, lanes] = (
                one * rows_of + two * ahead(rows_of, 1, rim) + three * ahead(rows_of, 2, rim)
            ).astype(bf16)
        if (start + chunk) % slices[0].size == 0:
            at = start // slices[0].size
            for which in range(4):
                part = (slice(None), slices[at])
                copy = pltpu.make_async_copy(
                    held[which].at[part], targets[which].at[part], sems.at[at, which]
                )
                copy.start()
                copies.append(copy)
    for copy in copies:
        copy.wait()


def local(query_in, key_in, value_in, conv_taps, long_filter, skip_gain, grad_out):
    rows, channels = query_in.shape
    blocks = lax.axis_size("inner") * lax.axis_size("outer")
    width = channels // blocks
    unit = 8 if width % 8 == 0 else width
    groups = width // unit
    large = pltpu.CompilerParams(vmem_limit_bytes=60 * 1024 * 1024)
    small = pltpu.CompilerParams(vmem_limit_bytes=24 * 1024 * 1024) if unit == 8 else large
    skip = skip_gain.reshape(1, channels)

    run = min(width, 2 * unit)
    own = conv_taps.reshape(3, 3, width // run, blocks, run)
    own = lax.dynamic_index_in_dim(own, lax.axis_index(AXES), 3, keepdims=False)
    own = own.reshape(3, 3, groups, unit)
    own = jnp.stack([own[1], own[2], own[0]])
    own = jnp.repeat(jnp.transpose(own, (1, 3, 2, 0)), 2, axis=3)
    own = jnp.pad(own, ((0, 0), (0, 0), (0, 0), (0, ITEMS - 6))).reshape(3, unit, ITEMS * groups)
    own = jnp.pad(own, ((0, 0), (0, 0), (0, rows - ITEMS * groups)))

    far = pl.BlockSpec(memory_space=pltpu.HBM)
    near = pl.BlockSpec(memory_space=pltpu.VMEM)
    stream = pltpu.VMEM((rows, channels), bf16)
    parts = len(slices_of(channels))
    packed = pl.pallas_call(
        functools.partial(gate_kernel, unit),
        out_shape=jax.ShapeDtypeStruct((blocks, 3 * width + unit, rows), bf16),
        in_specs=[far] * 6,
        out_specs=far,
        scratch_shapes=[
            *[stream] * 4,
            pltpu.VMEM((rows, channels), f32),
            pltpu.VMEM((3, 3, channels), f32),
            pltpu.VMEM((blocks, 3 * width + unit, rows), bf16),
            pltpu.VMEM((ITEMS, channels), f32),
            pltpu.SemaphoreType.DMA((6,)),
            pltpu.SemaphoreType.DMA((2,)),
        ],
        compiler_params=large,
        name="gate",
    )(query_in, key_in, value_in, grad_out, long_filter, conv_taps)
    spread = lax.all_to_all(packed, AXES, 0, 0, tiled=True)
    *short, tail, ready = pl.pallas_call(
        prepare_kernel,
        out_shape=(
            jax.ShapeDtypeStruct((rows, channels), f32),
            jax.ShapeDtypeStruct((2, rows, channels), f32),
            jax.ShapeDtypeStruct((3, 8, channels), f32),
            jax.ShapeDtypeStruct((unit, rows), f32),
        ),
        compiler_params=large,
        cost_estimate=pl.CostEstimate(
            flops=30 * rows * channels, bytes_accessed=20 * rows * channels, transcendentals=0
        ),
        name="prepare",
    )(query_in, key_in, value_in, conv_taps)
    result = pl.pallas_call(
        functools.partial(transform_kernel, groups, width),
        out_shape=jax.ShapeDtypeStruct((blocks, 2 * width + unit, rows), bf16),
        in_specs=[near, near, near],
        compiler_params=small,
        name="transform",
    )(spread, own * ready, jnp.asarray(tables(blocks, rows, unit)))
    returned = lax.all_to_all(result, AXES, 0, 0, tiled=True)
    wide = jax.ShapeDtypeStruct((rows, channels), bf16)
    return pl.pallas_call(
        functools.partial(finish_kernel, unit),
        out_shape=(wide, wide, wide, wide),
        in_specs=[near] * 7,
        out_specs=(far, far, far, far),
        scratch_shapes=[*[stream] * 4, pltpu.SemaphoreType.DMA((parts, 4))],
        compiler_params=small,
        name="finish",
    )(returned, grad_out, *short, tail, conv_taps, skip)


def solution(mesh):
    split = P(AXES, None)
    return jax.shard_map(
        local,
        mesh=mesh,
        in_specs=(split, split, split, P(), split, P(), split),
        out_specs=(split, split, split, split),
        check_vma=False,
    )
```

```python
import functools
import math

import jax
import jax.numpy as jnp
import ml_dtypes
import numpy as np
from jax import lax
from jax.experimental import pallas as pl
from jax.experimental.pallas import tpu as pltpu
from jax.sharding import PartitionSpec as P

AXES = ("outer", "inner")
f32 = jnp.float32
bf16 = jnp.bfloat16
ITEMS = 32

REACH = 2.0 ** (126.0 / 17.0)


def scale_of(top):
    return jnp.maximum(top, 2.0**-100).astype(bf16).astype(f32)


def encode(value, scale):
    base = value * (REACH / scale)
    power = base
    for _ in range(4):
        power = power * power
    return power * base


def decode(word):
    size = jnp.maximum(jnp.abs(word), 2.0**-126)
    return word * jnp.exp2(jnp.log2(size) * (-16.0 / 17.0))


def split_pair(value):
    high = value.astype(bf16)
    return high, (value - high.astype(f32)).astype(bf16)


def numpy_pair(value):
    high = value.astype(np.float32).astype(ml_dtypes.bfloat16)
    low = (value - high.astype(np.float64)).astype(np.float32).astype(ml_dtypes.bfloat16)
    return high, low


def table_on_left(table, value):
    high, low = split_pair(value)
    return jnp.dot(table, jnp.concatenate([high, low, high], axis=0), preferred_element_type=f32)


def table_on_right(value, high_table, low_table):
    high, low = split_pair(value)
    table = jnp.concatenate([high_table, low_table, high_table], axis=0)
    return jnp.dot(jnp.concatenate([high, high, low], axis=1), table, preferred_element_type=f32)


@functools.lru_cache(maxsize=None)
def tables(blocks, rows, unit):
    points = 2 * blocks * rows
    bins = 2 * np.arange(blocks // 4) + 1
    eye = np.eye(unit)
    coarse, coarse_back = [], []
    for which in range(4):
        angle = np.outer(bins, np.arange(which, blocks, 4)) * (math.pi / (2 * blocks))
        parts = [np.kron(np.cos(angle), eye), np.kron(-np.sin(angle), eye)]
        coarse.append(np.concatenate(parts, axis=0))
        coarse_back.append(np.concatenate([part.T for part in parts], axis=1) * (2.0 / points))
    signed = np.concatenate([bins, blocks + bins, bins - blocks, bins - 2 * blocks])
    twist = np.repeat(np.outer(signed, np.arange(rows)) * (math.pi / points), unit, axis=0)
    fine = np.outer(np.arange(rows), np.arange(rows)) * (2 * math.pi / rows)
    cos, sin = np.cos(fine), np.sin(fine)
    forward = np.block([[cos, -sin], [sin, cos]])
    backward = np.block([[cos, sin], [-sin, cos]])
    twists = np.concatenate([np.cos(twist), np.sin(twist)], axis=1)
    whole = []
    for table in coarse + coarse_back:
        high, low = numpy_pair(table)
        whole.append(np.concatenate([high, high, low], axis=1))
    for table in (forward, backward, twists):
        whole += numpy_pair(table)
    columns, flat = 2 * rows, []
    for table in whole:
        wide = np.pad(table, ((0, 0), (0, -table.shape[1] % columns)))
        flat += np.split(wide, wide.shape[1] // columns, axis=1)
    return np.concatenate(flat)


def unpack_tables(ref, count, rows):
    columns, quarter = 2 * rows, count // 4
    shapes = [(2 * quarter, 3 * quarter)] * 4 + [(quarter, 6 * quarter)] * 4
    shapes += [(columns, columns)] * 4 + [(count, columns)] * 2
    found, at = [], 0
    for height, length in shapes:
        parts = []
        for start in range(0, length, columns):
            parts.append(ref[at : at + height, : min(columns, length - start)])
            at += height
        found.append(jnp.concatenate(parts, axis=1) if len(parts) > 1 else parts[0])
    twists = found[12].astype(f32) + found[13].astype(f32)
    return found[:4], found[4:8], found[8:10], found[10:12], twists[:, :rows], twists[:, rows:]


def coarse_forward(coarse, value, blocks, unit):
    sums = []
    for which in range(4):
        places = range(which * unit, blocks * unit, 4 * unit)
        part = jnp.concatenate([value[at : at + unit] for at in places], axis=0)
        total = table_on_left(coarse[which], part)
        half = total.shape[0] // 2
        sums.append((total[:half], total[half:]))
    even = [left + right for left, right in zip(sums[0], sums[2])]
    even_less = [left - right for left, right in zip(sums[0], sums[2])]
    odd = [left + right for left, right in zip(sums[1], sums[3])]
    odd_less = [left - right for left, right in zip(sums[1], sums[3])]
    real = [even[0] + odd[0], even_less[0] + odd_less[1], even_less[0] - odd_less[1], even[0] - odd[0]]
    imag = [even[1] + odd[1], even_less[1] - odd_less[0], even_less[1] + odd_less[0], even[1] - odd[1]]
    return jnp.concatenate(real, axis=0), jnp.concatenate(imag, axis=0)


def coarse_backward(coarse_back, real, imag, blocks, unit):
    quarter = blocks * unit // 4
    real = [real[at * quarter : (at + 1) * quarter] for at in range(4)]
    imag = [imag[at * quarter : (at + 1) * quarter] for at in range(4)]
    outer_real, outer_imag = real[0] + real[3], imag[0] + imag[3]
    inner_real, inner_imag = real[1] + real[2], imag[1] + imag[2]
    outer_real_less, outer_imag_less = real[0] - real[3], imag[0] - imag[3]
    inner_real_less, inner_imag_less = real[1] - real[2], imag[1] - imag[2]
    mixes = (
        (outer_real + inner_real, outer_imag + inner_imag),
        (outer_real_less - inner_imag_less, outer_imag_less + inner_real_less),
        (outer_real - inner_real, outer_imag - inner_imag),
        (outer_real_less + inner_imag_less, outer_imag_less - inner_real_less),
    )
    results = [
        table_on_left(coarse_back[which], jnp.concatenate(mix, axis=0))
        for which, mix in enumerate(mixes)
    ]
    pieces = []
    for block in range(blocks):
        at = block // 4 * unit
        pieces.append(results[block % 4][at : at + unit])
    return jnp.concatenate(pieces, axis=0)


def shifted(stream, steps, rim):
    rolled = pltpu.roll(stream, steps, 0)
    if rim is None:
        return rolled
    edge = rolled[:8]
    row = lax.broadcasted_iota(jnp.int32, edge.shape, 0)
    for at in range(steps):
        edge = jnp.where(row == at, rim[2 - steps + at : 3 - steps + at], edge)
    return jnp.concatenate([edge, rolled[8:]], axis=0)


def short_forward(stream, taps, rim):
    return taps[0] * stream + taps[1] * shifted(stream, 1, rim) + taps[2] * shifted(stream, 2, rim)


def short_after(stream, following, taps):
    window = jnp.concatenate([stream[stream.shape[0] - 2 :], following], axis=0)
    return taps[0] * window[2:4] + taps[1] * window[1:3] + taps[2] * window[0:2]


def taps_at(taps_ref, which, lanes):
    return [taps_ref[which, tap : tap + 1, lanes] for tap in range(3)]


def ahead(rows, steps, rim):
    count = rows.shape[0]
    rolled = pltpu.roll(rows, count - steps, 0)
    edge = rolled[count - 8 :]
    row = lax.broadcasted_iota(jnp.int32, edge.shape, 0)
    for at in range(steps):
        edge = jnp.where(row == 8 - steps + at, rim[at : at + 1], edge)
    return jnp.concatenate([rolled[: count - 8], edge], axis=0)


def slices_of(channels):
    size = min(512, channels)
    return [pl.ds(start, size) for start in range(0, channels, size)]


def gate_kernel(unit, q_hbm, k_hbm, v_hbm, g_hbm, h_hbm, taps_hbm, out_hbm, *scratch):
    q_ref, k_ref, v_ref, g_ref, h_ref, taps_ref, out_ref, extra, sems, out_sems = scratch
    rows, channels = q_ref.shape
    blocks = out_ref.shape[0]
    width = channels // blocks
    run = min(width, 2 * unit)
    span = run * blocks
    chunk = 128
    pairs = (
        (taps_hbm, taps_ref),
        (k_hbm, k_ref),
        (v_hbm, v_ref),
        (q_hbm, q_ref),
        (g_hbm, g_ref),
        (h_hbm, h_ref),
    )
    copies = [
        pltpu.make_async_copy(hbm, ref, sems.at[at]) for at, (hbm, ref) in enumerate(pairs)
    ]
    for copy in copies:
        copy.start()
    extra[14:ITEMS, :] = jnp.zeros((ITEMS - 14, channels), f32)
    row = lax.broadcasted_iota(jnp.int32, (8, chunk), 0)

    def short(ref, tap_row, item, lanes):
        stream = ref[:, lanes].astype(f32)
        extra[2 * item : 2 * item + 2, lanes] = stream[0:2]
        extra[8 + 2 * item : 10 + 2 * item, lanes] = stream[rows - 2 :]
        return short_forward(stream, taps_at(taps_ref, tap_row, lanes), None)

    def send(which, start, signal):
        lanes = pl.ds(start, chunk)
        first, line = start % span // run, start // span * run
        if which != 1:
            edge = jnp.where(row < 2, 0.0, signal[:8])
            signal = jnp.concatenate([edge, signal[8:]], axis=0)
        scale = scale_of(jnp.max(jnp.abs(signal), axis=0, keepdims=True))
        extra[14 + which : 15 + which, lanes] = scale
        words = encode(signal, scale)
        if run % 16 == 0:
            words = words.astype(bf16).T.reshape(chunk // run, run, rows)
        else:
            words = words.T.reshape(chunk // run, run, rows).astype(bf16)
        out_ref[pl.ds(first, chunk // run), pl.ds(which * width + line, run), :] = words

    halves = run // unit
    waited = []

    def wait_for(*which):
        for at in which:
            if at not in waited:
                copies[at].wait()
                waited.append(at)

    outs = []
    for part in range(2):
        half_span = span // 2
        firsts = [at + part * half_span for at in range(0, channels, span)]
        starts = [first + at for first in firsts for at in range(0, half_span, chunk)]
        wait_for(0, 1, 2)
        for start in starts:
            lanes = pl.ds(start, chunk)
            send(0, start, short(k_ref, 1, 0, lanes) * short(v_ref, 2, 1, lanes))
        wait_for(3, 4)
        for start in starts:
            lanes = pl.ds(start, chunk)
            upstream = g_ref[:, lanes].astype(f32)
            extra[6:8, lanes] = upstream[0:2]
            send(2, start, upstream * short(q_ref, 0, 2, lanes))
        wait_for(5)
        for start in starts:
            send(1, start, h_ref[:, pl.ds(start, chunk)])
        items = []
        for first in firsts:
            items += [extra[:, first : first + half_span]] * halves
        if ITEMS * len(items) < rows:
            items.append(jnp.zeros((rows - ITEMS * len(items), half_span), f32))
        lines = jnp.concatenate(items, axis=0).T.reshape(blocks // 2, run, rows)
        lane = lax.broadcasted_iota(jnp.int32, (blocks // 2, unit, rows), 2)
        merged = lines[:, :unit, :]
        for half in range(1, halves):
            other = lines[:, half * unit : (half + 1) * unit, :]
            merged = jnp.where(lane // ITEMS % halves == half, other, merged)
        mine = pl.ds(part * (blocks // 2), blocks // 2)
        out_ref[mine, 3 * width :, :] = merged.astype(bf16)
        copy = pltpu.make_async_copy(out_ref.at[mine], out_hbm.at[mine], out_sems.at[part])
        copy.start()
        outs.append(copy)
    for copy in outs:
        copy.wait()


def transform_kernel(groups, width, x_ref, own_ref, table_ref, out_ref):
    blocks, lines, rows = x_ref.shape
    unit = width // groups
    count = blocks * unit
    coarse, coarse_back, forward, backward, cos, sin = unpack_tables(table_ref, count, rows)
    together = 2 if groups % 2 == 0 else 1

    extra = x_ref[:, 3 * width :, :].astype(f32).reshape(count, rows)
    none = jnp.zeros((unit, rows), f32)
    before = jnp.concatenate([none, extra[: count - unit]], axis=0)
    after = jnp.concatenate([extra[unit:], none], axis=0)
    lane = lax.broadcasted_iota(jnp.int32, (count, rows), 1)
    item = lane % ITEMS

    def turn(value, steps):
        return value if steps % rows == 0 else pltpu.roll(value, steps % rows, 1)

    def own(tap):
        return jnp.broadcast_to(own_ref[tap][None], (blocks, unit, rows)).reshape(count, rows)

    middle = jnp.where(item % 2 == 0, turn(before, -9), turn(extra, 1))
    shorts = own(0) * extra + own(1) * middle + own(2) * turn(before, -8)
    edge_gated = shorts * turn(shorts, -2)
    edge_mixed = shorts * turn(extra, -2)

    def take(which, base):
        both = x_ref[:, pl.ds(which * width + base * unit, together * unit), :].astype(f32)
        signals = []
        for at in range(together):
            part = both[:, at * unit : (at + 1) * unit, :].reshape(count, rows)
            left = ITEMS * (base + at)
            scale = extra[:, left + 14 + which : left + 15 + which] * (1.0 / REACH)
            signal = decode(part) * scale
            if which == 0:
                signal = jnp.where(lane < 2, turn(edge_gated, -left), signal)
            if which == 2:
                signal = jnp.where(lane < 2, turn(edge_mixed, -left - 4), signal)
            signals.append(signal)
        return signals

    placed = jnp.zeros((count, rows), f32)
    for base in range(0, groups, together):
        taken = [take(which, base) for which in range(3)]
        stacked = jnp.concatenate(
            [taken[which][at] for at in range(together) for which in range(3)], axis=1
        )
        first_real, first_imag = coarse_forward(coarse, stacked, blocks, unit)
        lasts = []
        for at in range(together):
            spectra = []
            for which in range(3):
                here = slice((3 * at + which) * rows, (3 * at + which + 1) * rows)
                real, imag = first_real[:, here], first_imag[:, here]
                turned = jnp.concatenate(
                    [real * cos + imag * sin, imag * cos - real * sin], axis=1
                )
                spectrum = table_on_right(turned, *forward)
                spectra.append((spectrum[:, :rows], spectrum[:, rows:]))
            (gr, gi), (hr, hi), (mr, mi) = spectra
            for real, imag in (
                (gr * hr - gi * hi, gr * hi + gi * hr),
                (mr * hr + mi * hi, mi * hr - mr * hi),
            ):
                product = jnp.concatenate([real, imag], axis=1)
                plain = table_on_right(product, *backward)
                real, imag = plain[:, :rows], plain[:, rows:]
                lasts.append((real * cos - imag * sin, imag * cos + real * sin))
        real, imag = (jnp.concatenate(parts, axis=1) for parts in zip(*lasts))
        result = coarse_backward(coarse_back, real, imag, blocks, unit)
        for which in range(2):
            pieces = []
            for at in range(together):
                here = slice((2 * at + which) * rows, (2 * at + which + 1) * rows)
                part = result[:, here].reshape(blocks, unit, rows)
                scale = scale_of(
                    jnp.max(jnp.max(jnp.abs(part), axis=0), axis=1, keepdims=True)
                )
                words = encode(part, scale[None])
                pieces.append(words)
                left = ITEMS * (base + at) + 16 + 2 * which
                mine = turn(words.reshape(count, rows), left)
                placed = jnp.where((lane >= left) & (lane < left + 2), mine, placed)
                spot = ITEMS * (base + at) + 20 + which
                all_scale = jnp.broadcast_to(scale[None], (blocks, unit, rows))
                placed = jnp.where(lane == spot, all_scale.reshape(count, rows), placed)
            out_ref[:, pl.ds(which * width + base * unit, together * unit), :] = jnp.concatenate(
                pieces, axis=1
            ).astype(bf16)
    following = jnp.concatenate([placed[unit:], none], axis=0)
    placed = jnp.where(item < 20, following, placed)
    lines = jnp.where(item < 8, after, jnp.where(item < 14, before, placed))
    out_ref[:, 2 * width :, :] = lines.reshape(blocks, unit, rows).astype(bf16)


def prepare_kernel(q_ref, k_ref, v_ref, taps_ref, sq_ref, skv_ref, tail_ref, ready_ref):
    rows, channels = q_ref.shape
    chunk = 128
    none = jnp.zeros((2, chunk), f32)
    ready_ref[...] = jnp.ones(ready_ref.shape, f32)
    for start in range(0, channels, chunk):
        lanes = pl.ds(start, chunk)
        for which, ref in enumerate((q_ref, k_ref, v_ref)):
            stream = ref[:, lanes].astype(f32)
            tail_ref[which, :, lanes] = stream[rows - 8 :]
            target = sq_ref if which == 0 else skv_ref.at[which - 1]
            target[:, lanes] = short_forward(stream, taps_at(taps_ref, which, lanes), none)


def finish_kernel(
    unit, y_ref, g_ref, sq_ref, skv_ref, tail_ref, taps_ref, skip_ref, *refs
):
    targets, held, sems = refs[:4], refs[4:8], refs[8]
    rows, channels = g_ref.shape
    blocks = y_ref.shape[0]
    width = channels // blocks
    run = min(width, 2 * unit)
    span = run * blocks
    chunk = 128
    halves = run // unit
    slices = slices_of(channels)
    copies = []
    extra = y_ref[:, 2 * width :, :].astype(f32).reshape(blocks * unit, rows)
    parts = [extra] + [pltpu.roll(extra, rows - half * ITEMS, 1) for half in range(1, halves)]
    parts = [part.reshape(blocks, unit, rows) for part in parts]
    extra = jnp.concatenate(parts, axis=1).reshape(span, rows).T
    row = lax.broadcasted_iota(jnp.int32, (8, chunk), 0)
    for start in range(0, channels, chunk):
        lanes = pl.ds(start, chunk)
        first, line = start % span // run, start // span * run
        skip = skip_ref[:, lanes]
        top, inner = start // span * halves * ITEMS, start % span
        items = extra[top : top + ITEMS, inner : inner + chunk]
        after = [items[2 * at : 2 * at + 2] for at in range(4)]
        before = [items[8 + 2 * at : 10 + 2 * at] for at in range(3)]

        def arrived(which):
            part = y_ref[pl.ds(first, chunk // run), pl.ds(which * width + line, run), :]
            if run % 16 == 0:
                part = part.reshape(chunk, rows).T.astype(f32)
            else:
                part = part.astype(f32).reshape(chunk, rows).T
            scale = items[20 + which : 21 + which] * (1.0 / REACH)
            return decode(part) * scale, decode(items[16 + 2 * which : 18 + 2 * which]) * scale

        upstream = g_ref[:, lanes].astype(f32)
        taps = [taps_at(taps_ref, which, lanes) for which in range(3)]
        shorts = []
        for which, at in ((0, 2), (1, 0), (2, 1)):
            one, two, three = taps[which]
            past = before[at]
            short = sq_ref[:, lanes] if which == 0 else skv_ref[which - 1, :, lanes]
            edge = short[:8] + jnp.where(
                row == 0,
                two * past[1:2] + three * past[0:1],
                jnp.where(row == 1, three * past[1:2], 0.0),
            )
            tail = tail_ref[which, :, lanes]
            shorts.append(
                (
                    jnp.concatenate([edge, short[8:]], axis=0),
                    short_after(tail, after[at], taps[which]),
                )
            )
        results = (arrived(0), arrived(1))
        upstreams = (upstream, after[3])
        grads = [[], [], []]
        for here in range(2):
            short_q, short_k, short_v = (short[here] for short in shorts)
            mixed = results[0][here] + skip * (short_k * short_v)
            if here == 0:
                held[0][:, lanes] = (short_q * mixed).astype(bf16)
            grad_gated = results[1][here] + skip * (upstreams[here] * short_q)
            grads[0].append(upstreams[here] * mixed)
            grads[1].append(grad_gated * short_v)
            grads[2].append(grad_gated * short_k)
        for which in range(3):
            rows_of, rim = grads[which]
            one, two, three = taps[which]
            held[1 + which][:, lanes] = (
                one * rows_of + two * ahead(rows_of, 1, rim) + three * ahead(rows_of, 2, rim)
            ).astype(bf16)
        if (start + chunk) % slices[0].size == 0:
            at = start // slices[0].size
            for which in range(4):
                part = (slice(None), slices[at])
                copy = pltpu.make_async_copy(
                    held[which].at[part], targets[which].at[part], sems.at[at, which]
                )
                copy.start()
                copies.append(copy)
    for copy in copies:
        copy.wait()


def local(query_in, key_in, value_in, conv_taps, long_filter, skip_gain, grad_out):
    rows, channels = query_in.shape
    blocks = lax.axis_size("inner") * lax.axis_size("outer")
    width = channels // blocks
    unit = 8 if width % 8 == 0 else width
    groups = width // unit
    large = pltpu.CompilerParams(vmem_limit_bytes=60 * 1024 * 1024)
    small = pltpu.CompilerParams(vmem_limit_bytes=24 * 1024 * 1024) if unit == 8 else large
    skip = skip_gain.reshape(1, channels)

    run = min(width, 2 * unit)
    own = conv_taps.reshape(3, 3, width // run, blocks, run)
    own = lax.dynamic_index_in_dim(own, lax.axis_index(AXES), 3, keepdims=False)
    own = own.reshape(3, 3, groups, unit)
    own = jnp.stack([own[1], own[2], own[0]])
    own = jnp.repeat(jnp.transpose(own, (1, 3, 2, 0)), 2, axis=3)
    own = jnp.pad(own, ((0, 0), (0, 0), (0, 0), (0, ITEMS - 6))).reshape(3, unit, ITEMS * groups)
    own = jnp.pad(own, ((0, 0), (0, 0), (0, rows - ITEMS * groups)))

    far = pl.BlockSpec(memory_space=pltpu.HBM)
    near = pl.BlockSpec(memory_space=pltpu.VMEM)
    stream = pltpu.VMEM((rows, channels), bf16)
    parts = len(slices_of(channels))
    packed = pl.pallas_call(
        functools.partial(gate_kernel, unit),
        out_shape=jax.ShapeDtypeStruct((blocks, 3 * width + unit, rows), bf16),
        in_specs=[far] * 6,
        out_specs=far,
        scratch_shapes=[
            *[stream] * 4,
            pltpu.VMEM((rows, channels), f32),
            pltpu.VMEM((3, 3, channels), f32),
            pltpu.VMEM((blocks, 3 * width + unit, rows), bf16),
            pltpu.VMEM((ITEMS, channels), f32),
            pltpu.SemaphoreType.DMA((6,)),
            pltpu.SemaphoreType.DMA((2,)),
        ],
        compiler_params=large,
        name="gate",
    )(query_in, key_in, value_in, grad_out, long_filter, conv_taps)
    spread = lax.all_to_all(packed, AXES, 0, 0, tiled=True)
    *short, tail, ready = pl.pallas_call(
        prepare_kernel,
        out_shape=(
            jax.ShapeDtypeStruct((rows, channels), f32),
            jax.ShapeDtypeStruct((2, rows, channels), f32),
            jax.ShapeDtypeStruct((3, 8, channels), f32),
            jax.ShapeDtypeStruct((unit, rows), f32),
        ),
        compiler_params=large,
        cost_estimate=pl.CostEstimate(
            flops=30 * rows * channels, bytes_accessed=20 * rows * channels, transcendentals=0
        ),
        name="prepare",
    )(query_in, key_in, value_in, conv_taps)
    result = pl.pallas_call(
        functools.partial(transform_kernel, groups, width),
        out_shape=jax.ShapeDtypeStruct((blocks, 2 * width + unit, rows), bf16),
        in_specs=[near, near, near],
        compiler_params=small,
        name="transform",
    )(spread, own * ready, jnp.asarray(tables(blocks, rows, unit)))
    returned = lax.all_to_all(result, AXES, 0, 0, tiled=True)
    wide = jax.ShapeDtypeStruct((rows, channels), bf16)
    return pl.pallas_call(
        functools.partial(finish_kernel, unit),
        out_shape=(wide, wide, wide, wide),
        in_specs=[near] * 7,
        out_specs=(far, far, far, far),
        scratch_shapes=[*[stream] * 4, pltpu.SemaphoreType.DMA((parts, 4))],
        compiler_params=small,
        name="finish",
    )(returned, grad_out, *short, tail, conv_taps, skip)


def solution(mesh):
    split = P(AXES, None)
    return jax.shard_map(
        local,
        mesh=mesh,
        in_specs=(split, split, split, P(), split, P(), split),
        out_specs=(split, split, split, split),
        check_vma=False,
    )
```

```python
import functools
import math

import jax
import jax.numpy as jnp
import ml_dtypes
import numpy as np
from jax import lax
from jax.experimental import pallas as pl
from jax.experimental.pallas import tpu as pltpu
from jax.sharding import PartitionSpec as P

AXES = ("outer", "inner")
f32 = jnp.float32
bf16 = jnp.bfloat16
ITEMS = 32

REACH = 2.0 ** (126.0 / 17.0)


def scale_of(top):
    top = jnp.maximum(top, 2.0**-100)
    high = top.astype(bf16).astype(f32)
    low = (top - high).astype(bf16).astype(f32)
    return high + low, high, low


def encode(value, scale):
    base = value * (REACH / scale)
    power = base
    for _ in range(4):
        power = power * power
    return power * base


def decode(word):
    size = jnp.maximum(jnp.abs(word), 2.0**-126)
    return word * jnp.exp2(jnp.log2(size) * (-16.0 / 17.0))


def split_pair(value):
    high = value.astype(bf16)
    return high, (value - high.astype(f32)).astype(bf16)


def numpy_pair(value):
    high = value.astype(np.float32).astype(ml_dtypes.bfloat16)
    low = (value - high.astype(np.float64)).astype(np.float32).astype(ml_dtypes.bfloat16)
    return high, low


def table_on_left(table, value):
    high, low = split_pair(value)
    return jnp.dot(table, jnp.concatenate([high, low, high], axis=0), preferred_element_type=f32)


def table_on_right(value, high_table, low_table):
    high, low = split_pair(value)
    table = jnp.concatenate([high_table, low_table, high_table], axis=0)
    return jnp.dot(jnp.concatenate([high, high, low], axis=1), table, preferred_element_type=f32)


@functools.lru_cache(maxsize=None)
def tables(blocks, rows, unit):
    points = 2 * blocks * rows
    bins = 2 * np.arange(blocks // 4) + 1
    eye = np.eye(unit)
    coarse, coarse_back = [], []
    for which in range(4):
        angle = np.outer(bins, np.arange(which, blocks, 4)) * (math.pi / (2 * blocks))
        parts = [np.kron(np.cos(angle), eye), np.kron(-np.sin(angle), eye)]
        coarse.append(np.concatenate(parts, axis=0))
        coarse_back.append(np.concatenate([part.T for part in parts], axis=1) * (2.0 / points))
    signed = np.concatenate([bins, blocks + bins, bins - blocks, bins - 2 * blocks])
    twist = np.repeat(np.outer(signed, np.arange(rows)) * (math.pi / points), unit, axis=0)
    fine = np.outer(np.arange(rows), np.arange(rows)) * (2 * math.pi / rows)
    cos, sin = np.cos(fine), np.sin(fine)
    forward = np.block([[cos, -sin], [sin, cos]])
    backward = np.block([[cos, sin], [-sin, cos]])
    twists = np.concatenate([np.cos(twist), np.sin(twist)], axis=1)
    whole = []
    for table in coarse + coarse_back:
        high, low = numpy_pair(table)
        whole.append(np.concatenate([high, high, low], axis=1))
    for table in (forward, backward, twists):
        whole += numpy_pair(table)
    columns, flat = 2 * rows, []
    for table in whole:
        wide = np.pad(table, ((0, 0), (0, -table.shape[1] % columns)))
        flat += np.split(wide, wide.shape[1] // columns, axis=1)
    return np.concatenate(flat)


def unpack_tables(ref, count, rows):
    columns, quarter = 2 * rows, count // 4
    shapes = [(2 * quarter, 3 * quarter)] * 4 + [(quarter, 6 * quarter)] * 4
    shapes += [(columns, columns)] * 4 + [(count, columns)] * 2
    found, at = [], 0
    for height, length in shapes:
        parts = []
        for start in range(0, length, columns):
            parts.append(ref[at : at + height, : min(columns, length - start)])
            at += height
        found.append(jnp.concatenate(parts, axis=1) if len(parts) > 1 else parts[0])
    twists = found[12].astype(f32) + found[13].astype(f32)
    return found[:4], found[4:8], found[8:10], found[10:12], twists[:, :rows], twists[:, rows:]


def coarse_forward(coarse, value, blocks, unit):
    sums = []
    for which in range(4):
        places = range(which * unit, blocks * unit, 4 * unit)
        part = jnp.concatenate([value[at : at + unit] for at in places], axis=0)
        total = table_on_left(coarse[which], part)
        half = total.shape[0] // 2
        sums.append((total[:half], total[half:]))
    even = [left + right for left, right in zip(sums[0], sums[2])]
    even_less = [left - right for left, right in zip(sums[0], sums[2])]
    odd = [left + right for left, right in zip(sums[1], sums[3])]
    odd_less = [left - right for left, right in zip(sums[1], sums[3])]
    real = [even[0] + odd[0], even_less[0] + odd_less[1], even_less[0] - odd_less[1], even[0] - odd[0]]
    imag = [even[1] + odd[1], even_less[1] - odd_less[0], even_less[1] + odd_less[0], even[1] - odd[1]]
    return jnp.concatenate(real, axis=0), jnp.concatenate(imag, axis=0)


def coarse_backward(coarse_back, real, imag, blocks, unit):
    quarter = blocks * unit // 4
    real = [real[at * quarter : (at + 1) * quarter] for at in range(4)]
    imag = [imag[at * quarter : (at + 1) * quarter] for at in range(4)]
    outer_real, outer_imag = real[0] + real[3], imag[0] + imag[3]
    inner_real, inner_imag = real[1] + real[2], imag[1] + imag[2]
    outer_real_less, outer_imag_less = real[0] - real[3], imag[0] - imag[3]
    inner_real_less, inner_imag_less = real[1] - real[2], imag[1] - imag[2]
    mixes = (
        (outer_real + inner_real, outer_imag + inner_imag),
        (outer_real_less - inner_imag_less, outer_imag_less + inner_real_less),
        (outer_real - inner_real, outer_imag - inner_imag),
        (outer_real_less + inner_imag_less, outer_imag_less - inner_real_less),
    )
    results = [
        table_on_left(coarse_back[which], jnp.concatenate(mix, axis=0))
        for which, mix in enumerate(mixes)
    ]
    pieces = []
    for block in range(blocks):
        at = block // 4 * unit
        pieces.append(results[block % 4][at : at + unit])
    return jnp.concatenate(pieces, axis=0)


def shifted(stream, steps, rim):
    rolled = pltpu.roll(stream, steps, 0)
    if rim is None:
        return rolled
    edge = rolled[:8]
    row = lax.broadcasted_iota(jnp.int32, edge.shape, 0)
    for at in range(steps):
        edge = jnp.where(row == at, rim[2 - steps + at : 3 - steps + at], edge)
    return jnp.concatenate([edge, rolled[8:]], axis=0)


def short_forward(stream, taps, rim):
    return taps[0] * stream + taps[1] * shifted(stream, 1, rim) + taps[2] * shifted(stream, 2, rim)


def short_after(stream, following, taps):
    window = jnp.concatenate([stream[stream.shape[0] - 2 :], following], axis=0)
    return taps[0] * window[2:4] + taps[1] * window[1:3] + taps[2] * window[0:2]


def taps_at(taps_ref, which, lanes):
    return [taps_ref[which, tap : tap + 1, lanes] for tap in range(3)]


def ahead(rows, steps, rim):
    count = rows.shape[0]
    rolled = pltpu.roll(rows, count - steps, 0)
    edge = rolled[count - 8 :]
    row = lax.broadcasted_iota(jnp.int32, edge.shape, 0)
    for at in range(steps):
        edge = jnp.where(row == 8 - steps + at, rim[at : at + 1], edge)
    return jnp.concatenate([rolled[: count - 8], edge], axis=0)


def slices_of(channels):
    size = min(512, channels)
    return [pl.ds(start, size) for start in range(0, channels, size)]


def gate_kernel(unit, q_hbm, k_hbm, v_hbm, g_hbm, h_hbm, taps_hbm, out_hbm, *scratch):
    q_ref, k_ref, v_ref, g_ref, h_ref, taps_ref, out_ref, extra, sems, out_sems = scratch
    rows, channels = q_ref.shape
    blocks = out_ref.shape[0]
    width = channels // blocks
    run = min(width, 2 * unit)
    span = run * blocks
    chunk = 128
    pairs = (
        (taps_hbm, taps_ref),
        (k_hbm, k_ref),
        (v_hbm, v_ref),
        (q_hbm, q_ref),
        (g_hbm, g_ref),
        (h_hbm, h_ref),
    )
    copies = [
        pltpu.make_async_copy(hbm, ref, sems.at[at]) for at, (hbm, ref) in enumerate(pairs)
    ]
    for copy in copies:
        copy.start()
    extra[14:ITEMS, :] = jnp.zeros((ITEMS - 14, channels), f32)
    row = lax.broadcasted_iota(jnp.int32, (8, chunk), 0)

    def short(ref, tap_row, item, lanes):
        stream = ref[:, lanes].astype(f32)
        extra[2 * item : 2 * item + 2, lanes] = stream[0:2]
        extra[8 + 2 * item : 10 + 2 * item, lanes] = stream[rows - 2 :]
        return short_forward(stream, taps_at(taps_ref, tap_row, lanes), None)

    def send(which, start, signal):
        lanes = pl.ds(start, chunk)
        first, line = start % span // run, start // span * run
        if which != 1:
            edge = jnp.where(row < 2, 0.0, signal[:8])
            signal = jnp.concatenate([edge, signal[8:]], axis=0)
        scale, high, low = scale_of(jnp.max(jnp.abs(signal), axis=0, keepdims=True))
        extra[14 + which : 15 + which, lanes] = high
        extra[17 + which : 18 + which, lanes] = low
        words = encode(signal, scale)
        if run % 16 == 0:
            words = words.astype(bf16).T.reshape(chunk // run, run, rows)
        else:
            words = words.T.reshape(chunk // run, run, rows).astype(bf16)
        out_ref[pl.ds(first, chunk // run), pl.ds(which * width + line, run), :] = words

    halves = run // unit
    waited = []

    def wait_for(*which):
        for at in which:
            if at not in waited:
                copies[at].wait()
                waited.append(at)

    outs = []
    for part in range(2):
        half_span = span // 2
        firsts = [at + part * half_span for at in range(0, channels, span)]
        starts = [first + at for first in firsts for at in range(0, half_span, chunk)]
        wait_for(0, 1, 2)
        for start in starts:
            lanes = pl.ds(start, chunk)
            send(0, start, short(k_ref, 1, 0, lanes) * short(v_ref, 2, 1, lanes))
        wait_for(3, 4)
        for start in starts:
            lanes = pl.ds(start, chunk)
            upstream = g_ref[:, lanes].astype(f32)
            extra[6:8, lanes] = upstream[0:2]
            send(2, start, upstream * short(q_ref, 0, 2, lanes))
        wait_for(5)
        for start in starts:
            send(1, start, h_ref[:, pl.ds(start, chunk)])
        items = []
        for first in firsts:
            items += [extra[:, first : first + half_span]] * halves
        if ITEMS * len(items) < rows:
            items.append(jnp.zeros((rows - ITEMS * len(items), half_span), f32))
        lines = jnp.concatenate(items, axis=0).T.reshape(blocks // 2, run, rows)
        lane = lax.broadcasted_iota(jnp.int32, (blocks // 2, unit, rows), 2)
        merged = lines[:, :unit, :]
        for half in range(1, halves):
            other = lines[:, half * unit : (half + 1) * unit, :]
            merged = jnp.where(lane // ITEMS % halves == half, other, merged)
        mine = pl.ds(part * (blocks // 2), blocks // 2)
        out_ref[mine, 3 * width :, :] = merged.astype(bf16)
        copy = pltpu.make_async_copy(out_ref.at[mine], out_hbm.at[mine], out_sems.at[part])
        copy.start()
        outs.append(copy)
    for copy in outs:
        copy.wait()


def transform_kernel(groups, width, x_ref, own_ref, table_ref, out_ref):
    blocks, lines, rows = x_ref.shape
    unit = width // groups
    count = blocks * unit
    coarse, coarse_back, forward, backward, cos, sin = unpack_tables(table_ref, count, rows)
    together = 2 if groups % 2 == 0 else 1

    extra = x_ref[:, 3 * width :, :].astype(f32).reshape(count, rows)
    none = jnp.zeros((unit, rows), f32)
    before = jnp.concatenate([none, extra[: count - unit]], axis=0)
    after = jnp.concatenate([extra[unit:], none], axis=0)
    lane = lax.broadcasted_iota(jnp.int32, (count, rows), 1)
    item = lane % ITEMS

    def turn(value, steps):
        return value if steps % rows == 0 else pltpu.roll(value, steps % rows, 1)

    def own(tap):
        return jnp.broadcast_to(own_ref[tap][None], (blocks, unit, rows)).reshape(count, rows)

    middle = jnp.where(item % 2 == 0, turn(before, -9), turn(extra, 1))
    shorts = own(0) * extra + own(1) * middle + own(2) * turn(before, -8)
    edge_gated = shorts * turn(shorts, -2)
    edge_mixed = shorts * turn(extra, -2)

    def take(which, base):
        both = x_ref[:, pl.ds(which * width + base * unit, together * unit), :].astype(f32)
        signals = []
        for at in range(together):
            part = both[:, at * unit : (at + 1) * unit, :].reshape(count, rows)
            left = ITEMS * (base + at)
            scale = extra[:, left + 14 + which : left + 15 + which]
            scale = (scale + extra[:, left + 17 + which : left + 18 + which]) * (1.0 / REACH)
            signal = decode(part) * scale
            if which == 0:
                signal = jnp.where(lane < 2, turn(edge_gated, -left), signal)
            if which == 2:
                signal = jnp.where(lane < 2, turn(edge_mixed, -left - 4), signal)
            signals.append(signal)
        return signals

    placed = jnp.zeros((count, rows), f32)
    for base in range(0, groups, together):
        taken = [take(which, base) for which in range(3)]
        stacked = jnp.concatenate(
            [taken[which][at] for at in range(together) for which in range(3)], axis=1
        )
        first_real, first_imag = coarse_forward(coarse, stacked, blocks, unit)
        lasts = []
        for at in range(together):
            spectra = []
            for which in range(3):
                here = slice((3 * at + which) * rows, (3 * at + which + 1) * rows)
                real, imag = first_real[:, here], first_imag[:, here]
                turned = jnp.concatenate(
                    [real * cos + imag * sin, imag * cos - real * sin], axis=1
                )
                spectrum = table_on_right(turned, *forward)
                spectra.append((spectrum[:, :rows], spectrum[:, rows:]))
            (gr, gi), (hr, hi), (mr, mi) = spectra
            for real, imag in (
                (gr * hr - gi * hi, gr * hi + gi * hr),
                (mr * hr + mi * hi, mi * hr - mr * hi),
            ):
                product = jnp.concatenate([real, imag], axis=1)
                plain = table_on_right(product, *backward)
                real, imag = plain[:, :rows], plain[:, rows:]
                lasts.append((real * cos - imag * sin, imag * cos + real * sin))
        real, imag = (jnp.concatenate(parts, axis=1) for parts in zip(*lasts))
        result = coarse_backward(coarse_back, real, imag, blocks, unit)
        for which in range(2):
            pieces = []
            for at in range(together):
                here = slice((2 * at + which) * rows, (2 * at + which + 1) * rows)
                part = result[:, here].reshape(blocks, unit, rows)
                scale, *halves = scale_of(
                    jnp.max(jnp.max(jnp.abs(part), axis=0), axis=1, keepdims=True)
                )
                words = encode(part, scale[None])
                pieces.append(words)
                left = ITEMS * (base + at) + 16 + 2 * which
                mine = turn(words.reshape(count, rows), left)
                placed = jnp.where((lane >= left) & (lane < left + 2), mine, placed)
                spot = lane - (ITEMS * (base + at) + 20 + which)
                for nth, half in enumerate(halves):
                    value = jnp.broadcast_to(half[None], (blocks, unit, rows))
                    placed = jnp.where(spot == 2 * nth, value.reshape(count, rows), placed)
            out_ref[:, pl.ds(which * width + base * unit, together * unit), :] = jnp.concatenate(
                pieces, axis=1
            ).astype(bf16)
    following = jnp.concatenate([placed[unit:], none], axis=0)
    placed = jnp.where(item < 20, following, placed)
    lines = jnp.where(item < 8, after, jnp.where(item < 14, before, placed))
    out_ref[:, 2 * width :, :] = lines.reshape(blocks, unit, rows).astype(bf16)


def prepare_kernel(q_ref, k_ref, v_ref, taps_ref, sq_ref, skv_ref, tail_ref, ready_ref):
    rows, channels = q_ref.shape
    chunk = 128
    none = jnp.zeros((2, chunk), f32)
    ready_ref[...] = jnp.ones(ready_ref.shape, f32)
    for start in range(0, channels, chunk):
        lanes = pl.ds(start, chunk)
        for which, ref in enumerate((q_ref, k_ref, v_ref)):
            stream = ref[:, lanes].astype(f32)
            tail_ref[which, :, lanes] = stream[rows - 8 :]
            target = sq_ref if which == 0 else skv_ref.at[which - 1]
            target[:, lanes] = short_forward(stream, taps_at(taps_ref, which, lanes), none)


def finish_kernel(
    unit, y_ref, g_ref, sq_ref, skv_ref, tail_ref, taps_ref, skip_ref, *refs
):
    targets, held, sems = refs[:4], refs[4:8], refs[8]
    rows, channels = g_ref.shape
    blocks = y_ref.shape[0]
    width = channels // blocks
    run = min(width, 2 * unit)
    span = run * blocks
    chunk = 128
    halves = run // unit
    slices = slices_of(channels)
    copies = []
    extra = y_ref[:, 2 * width :, :].astype(f32).reshape(blocks * unit, rows)
    parts = [extra] + [pltpu.roll(extra, rows - half * ITEMS, 1) for half in range(1, halves)]
    parts = [part.reshape(blocks, unit, rows) for part in parts]
    extra = jnp.concatenate(parts, axis=1).reshape(span, rows).T
    row = lax.broadcasted_iota(jnp.int32, (8, chunk), 0)
    for start in range(0, channels, chunk):
        lanes = pl.ds(start, chunk)
        first, line = start % span // run, start // span * run
        skip = skip_ref[:, lanes]
        top, inner = start // span * halves * ITEMS, start % span
        items = extra[top : top + ITEMS, inner : inner + chunk]
        after = [items[2 * at : 2 * at + 2] for at in range(4)]
        before = [items[8 + 2 * at : 10 + 2 * at] for at in range(3)]

        def arrived(which):
            part = y_ref[pl.ds(first, chunk // run), pl.ds(which * width + line, run), :]
            if run % 16 == 0:
                part = part.reshape(chunk, rows).T.astype(f32)
            else:
                part = part.astype(f32).reshape(chunk, rows).T
            scale = items[20 + which : 21 + which] + items[22 + which : 23 + which]
            scale = scale * (1.0 / REACH)
            return decode(part) * scale, decode(items[16 + 2 * which : 18 + 2 * which]) * scale

        upstream = g_ref[:, lanes].astype(f32)
        taps = [taps_at(taps_ref, which, lanes) for which in range(3)]
        shorts = []
        for which, at in ((0, 2), (1, 0), (2, 1)):
            one, two, three = taps[which]
            past = before[at]
            short = sq_ref[:, lanes] if which == 0 else skv_ref[which - 1, :, lanes]
            edge = short[:8] + jnp.where(
                row == 0,
                two * past[1:2] + three * past[0:1],
                jnp.where(row == 1, three * past[1:2], 0.0),
            )
            tail = tail_ref[which, :, lanes]
            shorts.append(
                (
                    jnp.concatenate([edge, short[8:]], axis=0),
                    short_after(tail, after[at], taps[which]),
                )
            )
        results = (arrived(0), arrived(1))
        upstreams = (upstream, after[3])
        grads = [[], [], []]
        for here in range(2):
            short_q, short_k, short_v = (short[here] for short in shorts)
            mixed = results[0][here] + skip * (short_k * short_v)
            if here == 0:
                held[0][:, lanes] = (short_q * mixed).astype(bf16)
            grad_gated = results[1][here] + skip * (upstreams[here] * short_q)
            grads[0].append(upstreams[here] * mixed)
            grads[1].append(grad_gated * short_v)
            grads[2].append(grad_gated * short_k)
        for which in range(3):
            rows_of, rim = grads[which]
            one, two, three = taps[which]
            held[1 + which][:, lanes] = (
                one * rows_of + two * ahead(rows_of, 1, rim) + three * ahead(rows_of, 2, rim)
            ).astype(bf16)
        if (start + chunk) % slices[0].size == 0:
            at = start // slices[0].size
            for which in range(4):
                part = (slice(None), slices[at])
                copy = pltpu.make_async_copy(
                    held[which].at[part], targets[which].at[part], sems.at[at, which]
                )
                copy.start()
                copies.append(copy)
    for copy in copies:
        copy.wait()


def local(query_in, key_in, value_in, conv_taps, long_filter, skip_gain, grad_out):
    rows, channels = query_in.shape
    blocks = lax.axis_size("inner") * lax.axis_size("outer")
    width = channels // blocks
    unit = 8 if width % 8 == 0 else width
    groups = width // unit
    large = pltpu.CompilerParams(vmem_limit_bytes=60 * 1024 * 1024)
    small = pltpu.CompilerParams(vmem_limit_bytes=24 * 1024 * 1024) if unit == 8 else large
    skip = skip_gain.reshape(1, channels)

    run = min(width, 2 * unit)
    own = conv_taps.reshape(3, 3, width // run, blocks, run)
    own = lax.dynamic_index_in_dim(own, lax.axis_index(AXES), 3, keepdims=False)
    own = own.reshape(3, 3, groups, unit)
    own = jnp.stack([own[1], own[2], own[0]])
    own = jnp.repeat(jnp.transpose(own, (1, 3, 2, 0)), 2, axis=3)
    own = jnp.pad(own, ((0, 0), (0, 0), (0, 0), (0, ITEMS - 6))).reshape(3, unit, ITEMS * groups)
    own = jnp.pad(own, ((0, 0), (0, 0), (0, rows - ITEMS * groups)))

    far = pl.BlockSpec(memory_space=pltpu.HBM)
    near = pl.BlockSpec(memory_space=pltpu.VMEM)
    stream = pltpu.VMEM((rows, channels), bf16)
    parts = len(slices_of(channels))
    packed = pl.pallas_call(
        functools.partial(gate_kernel, unit),
        out_shape=jax.ShapeDtypeStruct((blocks, 3 * width + unit, rows), bf16),
        in_specs=[far] * 6,
        out_specs=far,
        scratch_shapes=[
            *[stream] * 4,
            pltpu.VMEM((rows, channels), f32),
            pltpu.VMEM((3, 3, channels), f32),
            pltpu.VMEM((blocks, 3 * width + unit, rows), bf16),
            pltpu.VMEM((ITEMS, channels), f32),
            pltpu.SemaphoreType.DMA((6,)),
            pltpu.SemaphoreType.DMA((2,)),
        ],
        compiler_params=large,
        name="gate",
    )(query_in, key_in, value_in, grad_out, long_filter, conv_taps)
    spread = lax.all_to_all(packed, AXES, 0, 0, tiled=True)
    *short, tail, ready = pl.pallas_call(
        prepare_kernel,
        out_shape=(
            jax.ShapeDtypeStruct((rows, channels), f32),
            jax.ShapeDtypeStruct((2, rows, channels), f32),
            jax.ShapeDtypeStruct((3, 8, channels), f32),
            jax.ShapeDtypeStruct((unit, rows), f32),
        ),
        compiler_params=large,
        cost_estimate=pl.CostEstimate(
            flops=30 * rows * channels, bytes_accessed=20 * rows * channels, transcendentals=0
        ),
        name="prepare",
    )(query_in, key_in, value_in, conv_taps)
    result = pl.pallas_call(
        functools.partial(transform_kernel, groups, width),
        out_shape=jax.ShapeDtypeStruct((blocks, 2 * width + unit, rows), bf16),
        in_specs=[near, near, near],
        compiler_params=small,
        name="transform",
    )(spread, own * ready, jnp.asarray(tables(blocks, rows, unit)))
    returned = lax.all_to_all(result, AXES, 0, 0, tiled=True)
    wide = jax.ShapeDtypeStruct((rows, channels), bf16)
    return pl.pallas_call(
        functools.partial(finish_kernel, unit),
        out_shape=(wide, wide, wide, wide),
        in_specs=[near] * 7,
        out_specs=(far, far, far, far),
        scratch_shapes=[*[stream] * 4, pltpu.SemaphoreType.DMA((parts, 4))],
        compiler_params=small,
        name="finish",
    )(returned, grad_out, *short, tail, conv_taps, skip)


def solution(mesh):
    split = P(AXES, None)
    return jax.shard_map(
        local,
        mesh=mesh,
        in_specs=(split, split, split, P(), split, P(), split),
        out_specs=(split, split, split, split),
        check_vma=False,
    )
```

```python
import functools
import math

import jax
import jax.numpy as jnp
import ml_dtypes
import numpy as np
from jax import lax
from jax.experimental import pallas as pl
from jax.experimental.pallas import tpu as pltpu
from jax.sharding import PartitionSpec as P

AXES = ("outer", "inner")
f32 = jnp.float32
bf16 = jnp.bfloat16
ITEMS = 32

REACH = 2.0 ** (126.0 / 17.0)


def scale_of(top):
    top = jnp.maximum(top, 2.0**-100)
    high = top.astype(bf16).astype(f32)
    low = (top - high).astype(bf16).astype(f32)
    return high + low, high, low


def encode(value, scale):
    base = value * (REACH / scale)
    power = base
    for _ in range(4):
        power = power * power
    return power * base


def decode(word):
    size = jnp.maximum(jnp.abs(word), 2.0**-126)
    return word * jnp.exp2(jnp.log2(size) * (-16.0 / 17.0))


def split_pair(value):
    high = value.astype(bf16)
    return high, (value - high.astype(f32)).astype(bf16)


def numpy_pair(value):
    high = value.astype(np.float32).astype(ml_dtypes.bfloat16)
    low = (value - high.astype(np.float64)).astype(np.float32).astype(ml_dtypes.bfloat16)
    return high, low


def table_on_left(table, value):
    high, low = split_pair(value)
    return jnp.dot(table, jnp.concatenate([high, low, high], axis=0), preferred_element_type=f32)


def table_on_right(value, high_table, low_table):
    high, low = split_pair(value)
    table = jnp.concatenate([high_table, low_table, high_table], axis=0)
    return jnp.dot(jnp.concatenate([high, high, low], axis=1), table, preferred_element_type=f32)


@functools.lru_cache(maxsize=None)
def tables(blocks, rows, unit):
    points = 2 * blocks * rows
    bins = 2 * np.arange(blocks // 4) + 1
    eye = np.eye(unit)
    coarse, coarse_back = [], []
    for which in range(4):
        angle = np.outer(bins, np.arange(which, blocks, 4)) * (math.pi / (2 * blocks))
        parts = [np.kron(np.cos(angle), eye), np.kron(-np.sin(angle), eye)]
        coarse.append(np.concatenate(parts, axis=0))
        coarse_back.append(np.concatenate([part.T for part in parts], axis=1) * (2.0 / points))
    signed = np.concatenate([bins, blocks + bins, bins - blocks, bins - 2 * blocks])
    twist = np.repeat(np.outer(signed, np.arange(rows)) * (math.pi / points), unit, axis=0)
    fine = np.outer(np.arange(rows), np.arange(rows)) * (2 * math.pi / rows)
    cos, sin = np.cos(fine), np.sin(fine)
    forward = np.block([[cos, -sin], [sin, cos]])
    backward = np.block([[cos, sin], [-sin, cos]])
    twists = np.concatenate([np.cos(twist), np.sin(twist)], axis=1)
    whole = []
    for table in coarse + coarse_back:
        high, low = numpy_pair(table)
        whole.append(np.concatenate([high, high, low], axis=1))
    for table in (forward, backward, twists):
        whole += numpy_pair(table)
    columns, flat = 2 * rows, []
    for table in whole:
        wide = np.pad(table, ((0, 0), (0, -table.shape[1] % columns)))
        flat += np.split(wide, wide.shape[1] // columns, axis=1)
    return np.concatenate(flat)


def unpack_tables(ref, count, rows):
    columns, quarter = 2 * rows, count // 4
    shapes = [(2 * quarter, 3 * quarter)] * 4 + [(quarter, 6 * quarter)] * 4
    shapes += [(columns, columns)] * 4 + [(count, columns)] * 2
    found, at = [], 0
    for height, length in shapes:
        parts = []
        for start in range(0, length, columns):
            parts.append(ref[at : at + height, : min(columns, length - start)])
            at += height
        found.append(jnp.concatenate(parts, axis=1) if len(parts) > 1 else parts[0])
    twists = found[12].astype(f32) + found[13].astype(f32)
    return found[:4], found[4:8], found[8:10], found[10:12], twists[:, :rows], twists[:, rows:]


def coarse_forward(coarse, value, blocks, unit):
    sums = []
    for which in range(4):
        places = range(which * unit, blocks * unit, 4 * unit)
        part = jnp.concatenate([value[at : at + unit] for at in places], axis=0)
        total = table_on_left(coarse[which], part)
        half = total.shape[0] // 2
        sums.append((total[:half], total[half:]))
    even = [left + right for left, right in zip(sums[0], sums[2])]
    even_less = [left - right for left, right in zip(sums[0], sums[2])]
    odd = [left + right for left, right in zip(sums[1], sums[3])]
    odd_less = [left - right for left, right in zip(sums[1], sums[3])]
    real = [even[0] + odd[0], even_less[0] + odd_less[1], even_less[0] - odd_less[1], even[0] - odd[0]]
    imag = [even[1] + odd[1], even_less[1] - odd_less[0], even_less[1] + odd_less[0], even[1] - odd[1]]
    return jnp.concatenate(real, axis=0), jnp.concatenate(imag, axis=0)


def coarse_backward(coarse_back, real, imag, blocks, unit):
    quarter = blocks * unit // 4
    real = [real[at * quarter : (at + 1) * quarter] for at in range(4)]
    imag = [imag[at * quarter : (at + 1) * quarter] for at in range(4)]
    outer_real, outer_imag = real[0] + real[3], imag[0] + imag[3]
    inner_real, inner_imag = real[1] + real[2], imag[1] + imag[2]
    outer_real_less, outer_imag_less = real[0] - real[3], imag[0] - imag[3]
    inner_real_less, inner_imag_less = real[1] - real[2], imag[1] - imag[2]
    mixes = (
        (outer_real + inner_real, outer_imag + inner_imag),
        (outer_real_less - inner_imag_less, outer_imag_less + inner_real_less),
        (outer_real - inner_real, outer_imag - inner_imag),
        (outer_real_less + inner_imag_less, outer_imag_less - inner_real_less),
    )
    results = [
        table_on_left(coarse_back[which], jnp.concatenate(mix, axis=0))
        for which, mix in enumerate(mixes)
    ]
    pieces = []
    for block in range(blocks):
        at = block // 4 * unit
        pieces.append(results[block % 4][at : at + unit])
    return jnp.concatenate(pieces, axis=0)


def shifted(stream, steps, rim):
    rolled = pltpu.roll(stream, steps, 0)
    if rim is None:
        return rolled
    edge = rolled[:8]
    row = lax.broadcasted_iota(jnp.int32, edge.shape, 0)
    for at in range(steps):
        edge = jnp.where(row == at, rim[2 - steps + at : 3 - steps + at], edge)
    return jnp.concatenate([edge, rolled[8:]], axis=0)


def short_forward(stream, taps, rim):
    return taps[0] * stream + taps[1] * shifted(stream, 1, rim) + taps[2] * shifted(stream, 2, rim)


def short_after(stream, following, taps):
    window = jnp.concatenate([stream[stream.shape[0] - 2 :], following], axis=0)
    return taps[0] * window[2:4] + taps[1] * window[1:3] + taps[2] * window[0:2]


def taps_at(taps_ref, which, lanes):
    return [taps_ref[which, tap : tap + 1, lanes] for tap in range(3)]


def slices_of(channels):
    size = min(512, channels)
    return [pl.ds(start, size) for start in range(0, channels, size)]


def gate_kernel(unit, q_hbm, k_hbm, v_hbm, g_hbm, h_hbm, taps_hbm, out_hbm, *scratch):
    q_ref, k_ref, v_ref, g_ref, h_ref, taps_ref, out_ref, extra, sems, out_sems = scratch
    rows, channels = q_ref.shape
    blocks = out_ref.shape[0]
    width = channels // blocks
    run = min(width, 2 * unit)
    span = run * blocks
    chunk = 128
    pairs = (
        (taps_hbm, taps_ref),
        (k_hbm, k_ref),
        (v_hbm, v_ref),
        (q_hbm, q_ref),
        (g_hbm, g_ref),
        (h_hbm, h_ref),
    )
    copies = [
        pltpu.make_async_copy(hbm, ref, sems.at[at]) for at, (hbm, ref) in enumerate(pairs)
    ]
    for copy in copies:
        copy.start()
    extra[14:ITEMS, :] = jnp.zeros((ITEMS - 14, channels), f32)
    row = lax.broadcasted_iota(jnp.int32, (8, chunk), 0)

    def short(ref, tap_row, item, lanes):
        stream = ref[:, lanes].astype(f32)
        extra[2 * item : 2 * item + 2, lanes] = stream[0:2]
        extra[8 + 2 * item : 10 + 2 * item, lanes] = stream[rows - 2 :]
        return short_forward(stream, taps_at(taps_ref, tap_row, lanes), None)

    def send(which, start, signal):
        lanes = pl.ds(start, chunk)
        first, line = start % span // run, start // span * run
        if which != 1:
            edge = jnp.where(row < 2, 0.0, signal[:8])
            signal = jnp.concatenate([edge, signal[8:]], axis=0)
        scale, high, low = scale_of(jnp.max(jnp.abs(signal), axis=0, keepdims=True))
        extra[14 + which : 15 + which, lanes] = high
        extra[17 + which : 18 + which, lanes] = low
        words = encode(signal, scale)
        if run % 16 == 0:
            words = words.astype(bf16).T.reshape(chunk // run, run, rows)
        else:
            words = words.T.reshape(chunk // run, run, rows).astype(bf16)
        out_ref[pl.ds(first, chunk // run), pl.ds(which * width + line, run), :] = words

    halves = run // unit
    waited = []

    def wait_for(*which):
        for at in which:
            if at not in waited:
                copies[at].wait()
                waited.append(at)

    outs = []
    for part in range(2):
        half_span = span // 2
        firsts = [at + part * half_span for at in range(0, channels, span)]
        starts = [first + at for first in firsts for at in range(0, half_span, chunk)]
        wait_for(0, 1, 2)
        for start in starts:
            lanes = pl.ds(start, chunk)
            send(0, start, short(k_ref, 1, 0, lanes) * short(v_ref, 2, 1, lanes))
        wait_for(3, 4)
        for start in starts:
            lanes = pl.ds(start, chunk)
            upstream = g_ref[:, lanes].astype(f32)
            extra[6:8, lanes] = upstream[0:2]
            send(2, start, upstream * short(q_ref, 0, 2, lanes))
        wait_for(5)
        for start in starts:
            send(1, start, h_ref[:, pl.ds(start, chunk)])
        items = []
        for first in firsts:
            items += [extra[:, first : first + half_span]] * halves
        if ITEMS * len(items) < rows:
            items.append(jnp.zeros((rows - ITEMS * len(items), half_span), f32))
        lines = jnp.concatenate(items, axis=0).T.reshape(blocks // 2, run, rows)
        lane = lax.broadcasted_iota(jnp.int32, (blocks // 2, unit, rows), 2)
        merged = lines[:, :unit, :]
        for half in range(1, halves):
            other = lines[:, half * unit : (half + 1) * unit, :]
            merged = jnp.where(lane // ITEMS % halves == half, other, merged)
        mine = pl.ds(part * (blocks // 2), blocks // 2)
        out_ref[mine, 3 * width :, :] = merged.astype(bf16)
        copy = pltpu.make_async_copy(out_ref.at[mine], out_hbm.at[mine], out_sems.at[part])
        copy.start()
        outs.append(copy)
    for copy in outs:
        copy.wait()


def transform_kernel(groups, width, x_ref, own_ref, table_ref, out_ref):
    blocks, lines, rows = x_ref.shape
    unit = width // groups
    count = blocks * unit
    coarse, coarse_back, forward, backward, cos, sin = unpack_tables(table_ref, count, rows)
    together = 2 if groups % 2 == 0 else 1

    extra = x_ref[:, 3 * width :, :].astype(f32).reshape(count, rows)
    none = jnp.zeros((unit, rows), f32)
    before = jnp.concatenate([none, extra[: count - unit]], axis=0)
    after = jnp.concatenate([extra[unit:], none], axis=0)
    lane = lax.broadcasted_iota(jnp.int32, (count, rows), 1)
    item = lane % ITEMS

    def turn(value, steps):
        return value if steps % rows == 0 else pltpu.roll(value, steps % rows, 1)

    def own(tap):
        return jnp.broadcast_to(own_ref[tap][None], (blocks, unit, rows)).reshape(count, rows)

    middle = jnp.where(item % 2 == 0, turn(before, -9), turn(extra, 1))
    shorts = own(0) * extra + own(1) * middle + own(2) * turn(before, -8)
    edge_gated = shorts * turn(shorts, -2)
    edge_mixed = shorts * turn(extra, -2)

    def take(which, base):
        both = x_ref[:, pl.ds(which * width + base * unit, together * unit), :].astype(f32)
        signals = []
        for at in range(together):
            part = both[:, at * unit : (at + 1) * unit, :].reshape(count, rows)
            left = ITEMS * (base + at)
            scale = extra[:, left + 14 + which : left + 15 + which]
            scale = (scale + extra[:, left + 17 + which : left + 18 + which]) * (1.0 / REACH)
            signal = decode(part) * scale
            if which == 0:
                signal = jnp.where(lane < 2, turn(edge_gated, -left), signal)
            if which == 2:
                signal = jnp.where(lane < 2, turn(edge_mixed, -left - 4), signal)
            signals.append(signal)
        return signals

    placed = jnp.zeros((count, rows), f32)
    for base in range(0, groups, together):
        taken = [take(which, base) for which in range(3)]
        stacked = jnp.concatenate(
            [taken[which][at] for at in range(together) for which in range(3)], axis=1
        )
        first_real, first_imag = coarse_forward(coarse, stacked, blocks, unit)
        lasts = []
        for at in range(together):
            spectra = []
            for which in range(3):
                here = slice((3 * at + which) * rows, (3 * at + which + 1) * rows)
                real, imag = first_real[:, here], first_imag[:, here]
                turned = jnp.concatenate(
                    [real * cos + imag * sin, imag * cos - real * sin], axis=1
                )
                spectrum = table_on_right(turned, *forward)
                spectra.append((spectrum[:, :rows], spectrum[:, rows:]))
            (gr, gi), (hr, hi), (mr, mi) = spectra
            for real, imag in (
                (gr * hr - gi * hi, gr * hi + gi * hr),
                (mr * hr + mi * hi, mi * hr - mr * hi),
            ):
                product = jnp.concatenate([real, imag], axis=1)
                plain = table_on_right(product, *backward)
                real, imag = plain[:, :rows], plain[:, rows:]
                lasts.append((real * cos - imag * sin, imag * cos + real * sin))
        real, imag = (jnp.concatenate(parts, axis=1) for parts in zip(*lasts))
        result = coarse_backward(coarse_back, real, imag, blocks, unit)
        for which in range(2):
            pieces = []
            for at in range(together):
                here = slice((2 * at + which) * rows, (2 * at + which + 1) * rows)
                part = result[:, here].reshape(blocks, unit, rows)
                scale, *halves = scale_of(
                    jnp.max(jnp.max(jnp.abs(part), axis=0), axis=1, keepdims=True)
                )
                words = encode(part, scale[None])
                pieces.append(words)
                left = ITEMS * (base + at) + 16 + 2 * which
                mine = turn(words.reshape(count, rows), left)
                placed = jnp.where((lane >= left) & (lane < left + 2), mine, placed)
                spot = lane - (ITEMS * (base + at) + 20 + which)
                for nth, half in enumerate(halves):
                    value = jnp.broadcast_to(half[None], (blocks, unit, rows))
                    placed = jnp.where(spot == 2 * nth, value.reshape(count, rows), placed)
            out_ref[:, pl.ds(which * width + base * unit, together * unit), :] = jnp.concatenate(
                pieces, axis=1
            ).astype(bf16)
    following = jnp.concatenate([placed[unit:], none], axis=0)
    placed = jnp.where(item < 20, following, placed)
    lines = jnp.where(item < 8, after, jnp.where(item < 14, before, placed))
    out_ref[:, 2 * width :, :] = lines.reshape(blocks, unit, rows).astype(bf16)


def prepare_kernel(q_ref, k_ref, v_ref, taps_ref, sq_ref, skv_ref, tail_ref, ready_ref):
    rows, channels = q_ref.shape
    chunk = 128
    none = jnp.zeros((2, chunk), f32)
    ready_ref[...] = jnp.ones(ready_ref.shape, f32)
    for start in range(0, channels, chunk):
        lanes = pl.ds(start, chunk)
        for which, ref in enumerate((q_ref, k_ref, v_ref)):
            stream = ref[:, lanes].astype(f32)
            tail_ref[which, :, lanes] = stream[rows - 8 :]
            target = sq_ref if which == 0 else skv_ref.at[which - 1]
            target[:, lanes] = short_forward(stream, taps_at(taps_ref, which, lanes), none)


def finish_kernel(
    unit, y_ref, g_ref, sq_ref, skv_ref, tail_ref, taps_ref, skip_ref, *refs
):
    targets, held, sems, window = refs[:4], refs[4:8], refs[8], refs[9]
    rows, channels = g_ref.shape
    blocks = y_ref.shape[0]
    width = channels // blocks
    run = min(width, 2 * unit)
    span = run * blocks
    chunk = 128
    halves = run // unit
    slices = slices_of(channels)
    copies = []
    extra = y_ref[:, 2 * width :, :].astype(f32).reshape(blocks * unit, rows)
    parts = [extra] + [pltpu.roll(extra, rows - half * ITEMS, 1) for half in range(1, halves)]
    parts = [part.reshape(blocks, unit, rows) for part in parts]
    extra = jnp.concatenate(parts, axis=1).reshape(span, rows).T
    row = lax.broadcasted_iota(jnp.int32, (8, chunk), 0)
    for start in range(0, channels, chunk):
        lanes = pl.ds(start, chunk)
        first, line = start % span // run, start // span * run
        skip = skip_ref[:, lanes]
        top, inner = start // span * halves * ITEMS, start % span
        items = extra[top : top + ITEMS, inner : inner + chunk]
        after = [items[2 * at : 2 * at + 2] for at in range(4)]
        before = [items[8 + 2 * at : 10 + 2 * at] for at in range(3)]

        def arrived(which):
            part = y_ref[pl.ds(first, chunk // run), pl.ds(which * width + line, run), :]
            if run % 16 == 0:
                part = part.reshape(chunk, rows).T.astype(f32)
            else:
                part = part.astype(f32).reshape(chunk, rows).T
            scale = items[20 + which : 21 + which] + items[22 + which : 23 + which]
            scale = scale * (1.0 / REACH)
            return decode(part) * scale, decode(items[16 + 2 * which : 18 + 2 * which]) * scale

        upstream = g_ref[:, lanes].astype(f32)
        taps = [taps_at(taps_ref, which, lanes) for which in range(3)]
        shorts = []
        for which, at in ((0, 2), (1, 0), (2, 1)):
            one, two, three = taps[which]
            past = before[at]
            short = sq_ref[:, lanes] if which == 0 else skv_ref[which - 1, :, lanes]
            edge = short[:8] + jnp.where(
                row == 0,
                two * past[1:2] + three * past[0:1],
                jnp.where(row == 1, three * past[1:2], 0.0),
            )
            tail = tail_ref[which, :, lanes]
            shorts.append(
                (
                    jnp.concatenate([edge, short[8:]], axis=0),
                    short_after(tail, after[at], taps[which]),
                )
            )
        results = (arrived(0), arrived(1))
        upstreams = (upstream, after[3])
        grads = [[], [], []]
        for here in range(2):
            short_q, short_k, short_v = (short[here] for short in shorts)
            mixed = results[0][here] + skip * (short_k * short_v)
            if here == 0:
                held[0][:, lanes] = (short_q * mixed).astype(bf16)
            grad_gated = results[1][here] + skip * (upstreams[here] * short_q)
            grads[0].append(upstreams[here] * mixed)
            grads[1].append(grad_gated * short_v)
            grads[2].append(grad_gated * short_k)
        for which in range(3):
            rows_of, rim = grads[which]
            one, two, three = taps[which]
            view = window.at[start // chunk % 2 * 3 + which]
            view[:rows] = rows_of
            view[rows : rows + 2] = rim
            held[1 + which][:, lanes] = (
                one * rows_of + two * view[1 : rows + 1] + three * view[2 : rows + 2]
            ).astype(bf16)
        if (start + chunk) % slices[0].size == 0:
            at = start // slices[0].size
            for which in range(4):
                part = (slice(None), slices[at])
                copy = pltpu.make_async_copy(
                    held[which].at[part], targets[which].at[part], sems.at[at, which]
                )
                copy.start()
                copies.append(copy)
    for copy in copies:
        copy.wait()


def local(query_in, key_in, value_in, conv_taps, long_filter, skip_gain, grad_out):
    rows, channels = query_in.shape
    blocks = lax.axis_size("inner") * lax.axis_size("outer")
    width = channels // blocks
    unit = 8 if width % 8 == 0 else width
    groups = width // unit
    large = pltpu.CompilerParams(vmem_limit_bytes=60 * 1024 * 1024)
    small = pltpu.CompilerParams(vmem_limit_bytes=24 * 1024 * 1024) if unit == 8 else large
    skip = skip_gain.reshape(1, channels)

    run = min(width, 2 * unit)
    own = conv_taps.reshape(3, 3, width // run, blocks, run)
    own = lax.dynamic_index_in_dim(own, lax.axis_index(AXES), 3, keepdims=False)
    own = own.reshape(3, 3, groups, unit)
    own = jnp.stack([own[1], own[2], own[0]])
    own = jnp.repeat(jnp.transpose(own, (1, 3, 2, 0)), 2, axis=3)
    own = jnp.pad(own, ((0, 0), (0, 0), (0, 0), (0, ITEMS - 6))).reshape(3, unit, ITEMS * groups)
    own = jnp.pad(own, ((0, 0), (0, 0), (0, rows - ITEMS * groups)))

    far = pl.BlockSpec(memory_space=pltpu.HBM)
    near = pl.BlockSpec(memory_space=pltpu.VMEM)
    stream = pltpu.VMEM((rows, channels), bf16)
    parts = len(slices_of(channels))
    packed = pl.pallas_call(
        functools.partial(gate_kernel, unit),
        out_shape=jax.ShapeDtypeStruct((blocks, 3 * width + unit, rows), bf16),
        in_specs=[far] * 6,
        out_specs=far,
        scratch_shapes=[
            *[stream] * 4,
            pltpu.VMEM((rows, channels), f32),
            pltpu.VMEM((3, 3, channels), f32),
            pltpu.VMEM((blocks, 3 * width + unit, rows), bf16),
            pltpu.VMEM((ITEMS, channels), f32),
            pltpu.SemaphoreType.DMA((6,)),
            pltpu.SemaphoreType.DMA((2,)),
        ],
        compiler_params=large,
        name="gate",
    )(query_in, key_in, value_in, grad_out, long_filter, conv_taps)
    spread = lax.all_to_all(packed, AXES, 0, 0, tiled=True)
    *short, tail, ready = pl.pallas_call(
        prepare_kernel,
        out_shape=(
            jax.ShapeDtypeStruct((rows, channels), f32),
            jax.ShapeDtypeStruct((2, rows, channels), f32),
            jax.ShapeDtypeStruct((3, 8, channels), f32),
            jax.ShapeDtypeStruct((unit, rows), f32),
        ),
        compiler_params=large,
        cost_estimate=pl.CostEstimate(
            flops=30 * rows * channels, bytes_accessed=20 * rows * channels, transcendentals=0
        ),
        name="prepare",
    )(query_in, key_in, value_in, conv_taps)
    result = pl.pallas_call(
        functools.partial(transform_kernel, groups, width),
        out_shape=jax.ShapeDtypeStruct((blocks, 2 * width + unit, rows), bf16),
        in_specs=[near, near, near],
        compiler_params=small,
        name="transform",
    )(spread, own * ready, jnp.asarray(tables(blocks, rows, unit)))
    returned = lax.all_to_all(result, AXES, 0, 0, tiled=True)
    wide = jax.ShapeDtypeStruct((rows, channels), bf16)
    return pl.pallas_call(
        functools.partial(finish_kernel, unit),
        out_shape=(wide, wide, wide, wide),
        in_specs=[near] * 7,
        out_specs=(far, far, far, far),
        scratch_shapes=[
            *[stream] * 4,
            pltpu.SemaphoreType.DMA((parts, 4)),
            pltpu.VMEM((6, rows + 8, 128), f32),
        ],
        compiler_params=small,
        name="finish",
    )(returned, grad_out, *short, tail, conv_taps, skip)


def solution(mesh):
    split = P(AXES, None)
    return jax.shard_map(
        local,
        mesh=mesh,
        in_specs=(split, split, split, P(), split, P(), split),
        out_specs=(split, split, split, split),
        check_vma=False,
    )
```
